128 devices in a mesh: mem: 8 (over x_hi, y), tile: 16 (over x_lo, z, core).
Axes of the slice: x: 4 (x_hi: 2, x_lo: 2; x = x_hi * 2 + x_lo), y: 4, z: 4, core: 2. Of those that a mesh axis runs over, the one named last changes fastest.
Arguments:
- background_sample: bfloat16 [128, 227, 16384], P(('mem', 'tile')), may hold values from -6 to 6
- measured_reading: float32 [4, 512], replicated, may hold values from -8 to 8
- measurement_noise_variance: float32 [4, 512], replicated, may hold values from 0.25 to 1
- measurements_in_batch: int32 [4], replicated, may hold values from 256 to 512, as said below
- measurement_patch: int32 [4, 512, 1], replicated, may hold values from 0 to 127; in each aligned block of 512 rows (0 to 511, 512 to 1023, ..., all dimensions but the last counted through in order) at most 16 rows name the same one
- measurement_stack: int32 [4, 512], replicated, may hold values from 0 to 127
- measured_field: int32 [4, 512], replicated, may hold values from 0 to 226
- patch_measurement_roster: int32 [4, 128, 128], P(None, ('mem', 'tile')), may hold values from 0 to 511, as said below
- entry_damping_kind: int32 [4, 128, 128], P(None, ('mem', 'tile')), may hold values from 0 to 8
Outputs:
- analysis: bfloat16 [128, 227, 16384], P(None, None, ('mem', 'tile'))
The draws below stay inside these ranges and needn't reach their ends.
Inputs may be any that keep to these rules, and one draw needn't show every extreme that they name: A batch's first measurements_in_batch observations are in use; some batch uses all 512. `measurement_patch`: no tile holds more than 16 observations of one batch. `patch_measurement_roster`: the observations in one tile's list of one batch are distinct.
All inputs are finite; a program needn't handle non-finite values.
Results may differ from the reference program's by a relative error of at most 0.0023.
Values may be sent and summed in bfloat16 or wider, within the bound.
No kernel may reach another device: no remote copies, remote signals or barrier semaphores. Data moves between devices by JAX's collectives and lax.ppermute only.
A program may use at most 192 MiB of HBM per device.

```python
import math
import jax
import jax.numpy as jnp
import numpy as np
from jax import lax

FIELDS_PER_STACK = 227
STACKS_PER_PATCH = 128
BATCHES = 4
P_SIZE = 512
LMAX = 128
OWN_MAX = 16
CLASSES = 8
PATCH_NUMBER = 128
REALIZATIONS = 128
GRID_STACKS = 16384


def draw_measurements_in_batch(key, part):
    key = jax.random.fold_in(key, 11)
    first_key, second_key = jax.random.split(key)
    counts = jax.random.randint(first_key, (BATCHES,), P_SIZE // 2, P_SIZE + 1)
    full_batch = jax.random.randint(second_key, (), 0, BATCHES)
    return jnp.where(jnp.arange(BATCHES) == full_batch, P_SIZE, counts).astype(jnp.int32)


def draw_patch_measurement_roster(key, part):
    key = jax.random.fold_in(key, 23)
    row_keys = jax.random.split(key, BATCHES * PATCH_NUMBER)
    orders = jax.vmap(lambda row_key: jax.random.permutation(row_key, P_SIZE)[:LMAX])(row_keys)
    return orders.reshape(BATCHES, PATCH_NUMBER, LMAX).astype(jnp.int32)


def set_ends(array, key, smallest, high):
    longest = array.shape.index(max(array.shape))
    spots = []
    for shift in (0, 1):
        where = [jax.random.randint(jax.random.fold_in(key, axis), (), 0, length) for axis, length in enumerate(array.shape)]
        where[longest] = (where[longest] + shift) % array.shape[longest]
        spots.append(tuple(where))
    return array.at[spots[0]].set(smallest).at[spots[1]].set(high)


def steps_of(stream_key, extent, pieces, low, largest):
    level, own = 1.0, jax.random.fold_in(stream_key, 6)
    for position, parts in pieces:
        steps = jnp.exp(jax.random.uniform(jax.random.fold_in(own, position), (parts,), jnp.float32, low / len(pieces), largest / len(pieces)))
        level = level * jnp.repeat(steps, extent[position] // parts).reshape([-1 if axis == position else 1 for axis in range(len(extent))])
    return level


def assign_block(rng, own, number, rows, count, top, bound, slope):
    ranking = jax.random.permutation(rng, count)
    crowded, usual = portions_of(count, rows * top, bound, slope, True), portions_of(count, rows * top, bound, slope, False)
    places = jnp.arange(count)

    def named(sizes, offset_by):
        used = int((sizes > 0).sum())
        fixed = max(1, used // 4)
        moved = fixed + (places - fixed + offset_by * (used - fixed)) % max(1, count - fixed)
        return jnp.zeros((count,), jnp.int32).at[ranking[jnp.where(places < fixed, places, moved)]].set(jnp.asarray(sizes, jnp.int32))

    sizes = jnp.where(number % 4 == 0, named(crowded, number // 4), named(usual, number - number // 4 - 1))
    mixed = jax.random.permutation(jax.random.fold_in(own, 3), count)
    source_of, taker = mixed[0:count // 2 * 2:2], mixed[1:count // 2 * 2:2]
    slack = jnp.minimum(sizes[source_of] - 1, bound - sizes[taker]) // 2
    slack = jnp.where((source_of == ranking[0]) | (taker == ranking[0]) | (sizes[taker] == 0), 0, jnp.maximum(slack, 0))
    moved = jax.random.randint(jax.random.fold_in(own, 4), (count // 2,), 0, 1 << 20) % (slack + 1)
    sizes = sizes.at[source_of].add(-moved).at[taker].add(moved)
    items = jnp.searchsorted(jnp.cumsum(sizes), jnp.arange(rows * top), side="right").astype(jnp.int32)
    grid = items.reshape(top, rows).T
    grid = grid[jax.random.permutation(jax.random.fold_in(own, 1), rows)]
    offset_by = jax.random.randint(jax.random.fold_in(own, 2), (rows, 1), 0, top)
    return jnp.take_along_axis(grid, (jnp.arange(top)[None, :] + offset_by) % top, axis=1)


def portions_of(count, total, bound, slope, full):
    loads = [(1 << 20) // math.isqrt(standing ** slope) + 1 for standing in range(1, count + 1)]
    largest = bound if full else min(bound, max(-(-total // count), total * loads[0] // sum(loads)))
    least = 1 if total - largest >= count - 1 else 0
    holding, surplus = [largest] + [least] * (count - 1), total - largest - least * (count - 1)
    while surplus > 0:
        candidates = [i for i in range(1, count) if holding[i] < largest] or [i for i in range(1, count) if holding[i] < bound]
        whole, left = sum([loads[i] for i in candidates]), surplus
        for i in candidates:
            extra = min(bound - holding[i], max(1, left * loads[i] // whole), surplus)
            holding[i] = holding[i] + extra
            surplus = surplus - extra
    return np.array(holding)


def scatter_about(rng, dims, scale, reach, pieces=(), held_as=jnp.bfloat16):
    drawn = jax.random.normal(rng, dims, jnp.float32) * scale
    if len(pieces) > 0:
        drawn = steps_of(rng, dims, pieces, -0.22, 0.18) * drawn
    return jnp.clip(drawn, min=-reach, max=reach).astype(held_as)


def setup_inputs(seed: int = 0) -> dict:
    seeds = jax.random.split(jax.random.key(seed), 10)
    background_sample = scatter_about(seeds[0], (REALIZATIONS, FIELDS_PER_STACK, GRID_STACKS), 1.0, 6.0, ((0, 128),))
    measured_reading = scatter_about(seeds[1], (BATCHES, P_SIZE), 1.5, 8.0, (), jnp.float32)
    measurement_noise_variance = jnp.clip(jnp.exp(jax.random.uniform(seeds[2], (BATCHES, P_SIZE), jnp.float32, math.log(0.25), math.log(1.0))), 0.25, 1.0)
    measurements_in_batch = draw_measurements_in_batch(jax.random.fold_in(seeds[9], 71), 0)
    measurement_patch_keys = jax.random.split(jax.random.fold_in(seeds[4], 1), BATCHES * P_SIZE // P_SIZE)
    measurement_patch_turns = jax.random.permutation(jax.random.fold_in(seeds[4], 3), BATCHES * P_SIZE // P_SIZE)
    measurement_patch = jax.vmap(lambda own, number: assign_block(jax.random.fold_in(seeds[4], 2), own, number, P_SIZE, PATCH_NUMBER, 1, OWN_MAX, 2))(measurement_patch_keys, measurement_patch_turns).reshape((BATCHES, P_SIZE, 1))
    measurement_stack = set_ends(jax.random.randint(seeds[5], (BATCHES, P_SIZE), 0, STACKS_PER_PATCH), jax.random.fold_in(seeds[5], 1), 0, STACKS_PER_PATCH - 1).astype(jnp.int32)
    measured_field = set_ends(jax.random.randint(seeds[6], (BATCHES, P_SIZE), 0, FIELDS_PER_STACK), jax.random.fold_in(seeds[6], 1), 0, FIELDS_PER_STACK - 1).astype(jnp.int32)
    patch_measurement_roster = draw_patch_measurement_roster(jax.random.fold_in(seeds[9], 71), 0)
    entry_damping_kind = set_ends(jax.random.randint(seeds[8], (BATCHES, PATCH_NUMBER, LMAX), 0, CLASSES + 1), jax.random.fold_in(seeds[8], 1), 0, CLASSES).astype(jnp.int32)
    return {"background_sample": background_sample, "measured_reading": measured_reading, "measurement_noise_variance": measurement_noise_variance, "measurements_in_batch": measurements_in_batch, "measurement_patch": measurement_patch, "measurement_stack": measurement_stack, "measured_field": measured_field, "patch_measurement_roster": patch_measurement_roster, "entry_damping_kind": entry_damping_kind}


def analyse(realization_fields, prior_rows, weight, observed, variance):
    realization_number = realization_fields.shape[0]
    inverse_root = 1.0 / jnp.sqrt(jnp.float32(realization_number - 1))
    obs_mean = lax.optimization_barrier(jnp.mean(prior_rows, axis=1))
    scaled = weight[:, None] * (prior_rows - obs_mean[:, None]) * inverse_root
    innovation = weight * (observed - obs_mean)
    covariance = jnp.dot(scaled, scaled.T, precision=lax.Precision.HIGHEST) + jnp.diag(variance)
    factor = jnp.linalg.cholesky(covariance)
    solved = jax.scipy.linalg.cho_solve((factor, True), scaled)
    solved_d = jax.scipy.linalg.cho_solve((factor, True), innovation[:, None])
    mixing = jnp.dot(scaled.T, solved, precision=lax.Precision.HIGHEST)
    shift_vec = jnp.dot(scaled.T, solved_d, precision=lax.Precision.HIGHEST) * inverse_root
    transform = jnp.eye(realization_number, dtype=jnp.float32) - 0.5 * mixing + shift_vec
    centre = lax.optimization_barrier(jnp.mean(realization_fields, axis=0))
    spread = realization_fields - centre[None, :]
    return centre[None, :] + jnp.dot(transform.T, spread, precision=lax.Precision.HIGHEST)

def tapering(classes, listed, count):
    tapered = jnp.where(classes > 0, (CLASSES + 1 - classes).astype(jnp.float32) / CLASSES, jnp.float32(0.0))
    return tapered * (listed < count).astype(jnp.float32)

def reference(background_sample, measured_reading, measurement_noise_variance, measurements_in_batch, measurement_patch, measurement_stack, measured_field, patch_measurement_roster, entry_damping_kind):
    realization_fields = background_sample.reshape(REALIZATIONS, FIELDS_PER_STACK, PATCH_NUMBER, STACKS_PER_PATCH).transpose(2, 0, 1, 3).reshape(PATCH_NUMBER, REALIZATIONS, FIELDS_PER_STACK * STACKS_PER_PATCH).astype(jnp.float32)
    for batch_num in range(BATCHES):
        owner = measurement_patch[batch_num, :, 0]
        flat_index = measured_field[batch_num] * STACKS_PER_PATCH + measurement_stack[batch_num]
        prior = realization_fields[owner, :, flat_index]
        observed_all = measured_reading[batch_num]
        variance_all = measurement_noise_variance[batch_num]
        count = measurements_in_batch[batch_num]

        def one_tile(items):
            tile_state, listed, classes = items
            weight = tapering(classes, listed, count)
            return analyse(tile_state, prior[listed], weight, observed_all[listed], variance_all[listed])
        realization_fields = lax.map(one_tile, (realization_fields, patch_measurement_roster[batch_num], entry_damping_kind[batch_num]))
    return realization_fields.reshape(PATCH_NUMBER, REALIZATIONS, FIELDS_PER_STACK, STACKS_PER_PATCH).transpose(1, 2, 0, 3).reshape(REALIZATIONS, FIELDS_PER_STACK, GRID_STACKS).astype(jnp.bfloat16)
```

```python
import functools
import jax
import jax.numpy as jnp
from jax import lax
from jax.experimental import pallas as pl
from jax.experimental.pallas import tpu as pltpu
from jax.sharding import PartitionSpec as P

OWN_MAX = 16
CLASSES = 8
AXES = ("mem", "tile")
BATCHES = 4
OBS = 512
TILES = 128
MEMBERS = 128
LANES = 128
FIELDS = 227
SLOTS = BATCHES * OWN_MAX
GROUP = 8
VMEM_LIMIT = 48 * 1024 * 1024
HIGHEST = lax.Precision.HIGHEST
F32 = jnp.float32
BF16 = jnp.bfloat16
INVERSE_ROOT = 1.0 / (MEMBERS - 1) ** 0.5


def iota(shape, dim):
    return lax.broadcasted_iota(jnp.int32, shape, dim)


def dot(a, b, precision=None):
    return jnp.dot(a, b, precision=precision, preferred_element_type=F32)


def dot_nt(a, b):
    return lax.dot_general(a, b, (((1,), (1,)), ((), ())), preferred_element_type=F32)


def owner_order(owner_row):
    hot = iota((TILES, OBS), 0) == owner_row
    hot_f = jnp.where(hot, 1.0, 0.0)
    before = jnp.where(iota((OBS, OBS), 0) < iota((OBS, OBS), 1), 1.0, 0.0).astype(BF16)
    counts = dot(hot_f.astype(BF16), before)
    order = jnp.sum(hot_f * counts, axis=0, keepdims=True)
    return hot_f, order


def sort_out_kernel(x_ref, owner_ref, field_ref, stack_ref, blocks_ref, message_ref, table_ref, values_ref):
    step = pl.program_id(0)

    @pl.when(step == 0)
    def _():
        for b in range(BATCHES):
            hot, order = owner_order(owner_ref[b : b + 1, :])
            slot_hot = iota((OWN_MAX, OBS), 0).astype(F32) == order
            fields = jnp.where(slot_hot, field_ref[b : b + 1, :].astype(F32), 0.0).astype(BF16)
            stacks = jnp.where(slot_hot, stack_ref[b : b + 1, :].astype(F32), 0.0).astype(BF16)
            hot = hot.astype(BF16)
            table_ref[b * OWN_MAX : (b + 1) * OWN_MAX, :] = (
                dot_nt(fields, hot) * float(LANES) + dot_nt(stacks, hot)
            )
        values_ref[...] = jnp.zeros_like(values_ref)

    table = table_ref[...]
    lane_of = iota((SLOTS, LANES), 1)
    field_of = iota((SLOTS, FIELDS), 1)
    ones = jnp.ones((8, LANES), BF16)
    for i in range(GROUP):
        tile = step * GROUP + i
        block = x_ref[0, :, i * LANES : (i + 1) * LANES]
        blocks_ref[i] = block
        place = jnp.sum(jnp.where(lane_of == tile, table, 0.0), axis=1, keepdims=True).astype(jnp.int32)
        field = lax.shift_right_logical(place, 7)
        lane = lax.bitwise_and(place, LANES - 1)
        rows = dot(jnp.where(field_of == field, 1.0, 0.0).astype(BF16), block)
        picked = jnp.where(lane_of == lane, rows, 0.0).astype(BF16)
        values_ref[pl.ds(tile, 1), 0:SLOTS] = dot_nt(ones, picked)[0:1]

    @pl.when(step == pl.num_programs(0) - 1)
    def _():
        hot, order = owner_order(owner_ref[0:1, :])
        values = values_ref[...]
        turned = values.T[0:OWN_MAX].astype(BF16)
        by_slot = dot(turned, hot.astype(BF16))
        slot_hot = iota((OWN_MAX, OBS), 0).astype(F32) == order
        first = jnp.sum(jnp.where(slot_hot, by_slot, 0.0), axis=0, keepdims=True)
        parts = [
            jnp.broadcast_to(first[:, k * LANES : (k + 1) * LANES][None], (TILES, 1, LANES))
            for k in range(4)
        ]
        parts += [values[:, None, :], jnp.zeros((TILES, 3, LANES), F32)]
        message_ref[...] = jnp.concatenate(parts, axis=1).astype(BF16)


def sort_out(x, owner, field, stack):
    small = pl.BlockSpec((BATCHES, OBS), lambda i: (0, 0))
    return pl.pallas_call(
        sort_out_kernel,
        grid=(TILES // GROUP,),
        in_specs=[pl.BlockSpec((1, FIELDS, GROUP * LANES), lambda i: (0, 0, i)), small, small, small],
        out_specs=[
            pl.BlockSpec((GROUP, FIELDS, LANES), lambda i: (i, 0, 0)),
            pl.BlockSpec((TILES, 8, LANES), lambda i: (0, 0, 0)),
        ],
        out_shape=[
            jax.ShapeDtypeStruct((TILES, FIELDS, LANES), BF16),
            jax.ShapeDtypeStruct((TILES, 8, LANES), BF16),
        ],
        scratch_shapes=[pltpu.VMEM((SLOTS, LANES), F32), pltpu.VMEM((TILES, LANES), F32)],
        compiler_params=pltpu.CompilerParams(vmem_limit_bytes=VMEM_LIMIT),
    )(x, owner, field, stack)


def column(row):
    eye = iota((LANES, LANES), 0) == iota((LANES, LANES), 1)
    return jnp.broadcast_to(
        jnp.sum(jnp.where(eye, row, 0.0), axis=1, keepdims=True), (LANES, LANES)
    )


def lists_kernel(used_ref, owner_ref, roster_ref, kind_ref, reading_ref, variance_ref,
                 weight_ref, observed_ref, noise_ref, listed_ref, slot_ref):
    eye = iota((LANES, LANES), 0) == iota((LANES, LANES), 1)
    for b in range(BATCHES):
        listed = column(roster_ref[b].astype(F32))
        kind = column(kind_ref[b].astype(F32))
        listed_ref[b] = listed.astype(jnp.int32)
        taper = jnp.where(kind > 0.0, (CLASSES + 1 - kind) / CLASSES, 0.0)
        weight_ref[b] = jnp.where(listed < used_ref[b].astype(F32), taper, 0.0)
        _, order = owner_order(owner_ref[b : b + 1, :])
        slot = owner_ref[b : b + 1, :].astype(F32) * OWN_MAX + order
        wide = jnp.concatenate([listed] * (OBS // LANES), axis=1)
        hot = wide == iota((LANES, OBS), 1).astype(F32)

        def look_up(row):
            return jnp.sum(jnp.where(hot, row, 0.0), axis=1, keepdims=True)

        observed_ref[b] = jnp.broadcast_to(look_up(reading_ref[b : b + 1, :]), (LANES, LANES))
        noise_ref[b] = jnp.broadcast_to(look_up(variance_ref[b : b + 1, :]), (LANES, LANES))
        slots = jnp.sum(jnp.where(eye, look_up(slot), 0.0), axis=0, keepdims=True)
        slot_ref[b : b + 1, :] = slots.astype(jnp.int32)


def lists(used, owner, roster, kind, reading, variance):
    vmem = pl.BlockSpec(memory_space=pltpu.VMEM)
    square = jax.ShapeDtypeStruct((BATCHES, LANES, LANES), F32)
    return pl.pallas_call(
        lists_kernel,
        in_specs=[pl.BlockSpec(memory_space=pltpu.SMEM)] + [vmem] * 5,
        out_specs=[vmem] * 5,
        out_shape=[square, square, square, jax.ShapeDtypeStruct(square.shape, jnp.int32),
                   jax.ShapeDtypeStruct((BATCHES, LANES), jnp.int32)],
        compiler_params=pltpu.CompilerParams(vmem_limit_bytes=VMEM_LIMIT),
    )(used, owner, roster, kind, reading, variance)


def transform_of(prior, weight, observed, noise):
    eye = jnp.where(iota((LANES, LANES), 0) == iota((LANES, LANES), 1), 1.0, 0.0)
    mean = jnp.sum(prior, axis=1, keepdims=True) * (1.0 / MEMBERS)
    scaled = weight * (prior - mean) * INVERSE_ROOT
    inverse_noise = 1.0 / noise
    right = jnp.concatenate(
        [scaled * inverse_noise, weight * (observed - mean) * inverse_noise], axis=1
    )
    both = dot(scaled.T, right, HIGHEST)
    matrix = both[:, :LANES] + eye
    pull = both[:, LANES:]
    bound = jnp.max(jnp.sum(jnp.abs(matrix), axis=0, keepdims=True)) * 1.00001
    scale = 2.0 / (1.0 + bound)
    rho = (bound - 1.0) / (bound + 1.0)

    def unfinished(carry):
        return carry[0] > 1e-4

    def square(carry):
        rho, x, e = carry
        gain = 2.0 / (2.0 - rho * rho)
        products = dot(jnp.concatenate([x, e], axis=0), e, HIGHEST)
        x = gain * (x + products[:LANES])
        e = gain * products[LANES:] + (1.0 - gain) * eye
        return rho * rho / (2.0 - rho * rho), x, e

    _, inverse, _ = lax.while_loop(unfinished, square, (rho, scale * eye, eye - scale * matrix))

    def refine(_, x):
        return x + dot(x, eye - dot(matrix, x, HIGHEST), HIGHEST)

    inverse = lax.fori_loop(0, jnp.where(bound > 200.0, 2, 1), refine, inverse)
    return 0.5 * (eye + inverse) + dot(inverse, pull, HIGHEST) * INVERSE_ROOT


def first_kernel(message_ref, listed_ref, weight_ref, observed_ref, noise_ref,
                 sent_ref, own_ref, total_ref, scratch_ref):
    scratch_ref[...] = message_ref[...].astype(F32).reshape(MEMBERS * 8, LANES)
    listed = listed_ref[0]
    prior = jnp.zeros((LANES, MEMBERS), F32)
    for k in range(OBS // LANES):
        values = scratch_ref[pl.ds(k, MEMBERS, stride=8), :].astype(BF16)
        hot = jnp.where(listed == iota((LANES, LANES), 1) + k * LANES, 1.0, 0.0).astype(BF16)
        prior = prior + dot_nt(hot, values)
    own = scratch_ref[pl.ds(4, MEMBERS, stride=8), :].T[0:SLOTS]
    transform = transform_of(prior, weight_ref[0], observed_ref[0], noise_ref[0])
    own = dot(own, transform, HIGHEST)
    own_ref[...] = own
    total_ref[...] = transform
    sent_ref[...] = jnp.broadcast_to(own[OWN_MAX : 2 * OWN_MAX][None], (TILES, OWN_MAX, LANES))


def next_kernel(b, slot_ref, rows_ref, weight_ref, observed_ref, noise_ref, own_ref, total_ref,
                *outs):
    scratch_ref = outs[-1]
    for slot in range(LANES):
        scratch_ref[slot : slot + 1, :] = rows_ref[pl.ds(slot_ref[b, slot], 1), :]
    transform = transform_of(scratch_ref[...], weight_ref[0], observed_ref[0], noise_ref[0])
    if b < BATCHES - 1:
        sent_ref, own_out_ref, total_out_ref = outs[:-1]
        own = dot(own_ref[...], transform, HIGHEST)
        own_out_ref[...] = own
        total_out_ref[...] = dot(total_ref[...], transform, HIGHEST)
        sent = own[(b + 1) * OWN_MAX : (b + 2) * OWN_MAX]
        sent_ref[...] = jnp.broadcast_to(sent[None], (TILES, OWN_MAX, LANES))
    else:
        total = dot(total_ref[...], transform, HIGHEST).T
        high = total.astype(BF16)
        outs[0][:, :LANES] = high
        outs[0][:, LANES:] = (total - high.astype(F32)).astype(BF16)


def solve(b, source, slots, weight, observed, noise, own, total):
    vmem = pl.BlockSpec(memory_space=pltpu.VMEM)
    square = pl.BlockSpec((1, LANES, LANES), lambda i: (b, 0, 0))
    whole = lambda *shape: pl.BlockSpec(shape, lambda i: (0,) * len(shape))
    sent = jax.ShapeDtypeStruct((TILES, OWN_MAX, LANES), F32)
    owned = jax.ShapeDtypeStruct((SLOTS, LANES), F32)
    full = jax.ShapeDtypeStruct((LANES, LANES), F32)
    if b < BATCHES - 1:
        out_shape = [sent, owned, full]
    else:
        out_shape = [jax.ShapeDtypeStruct((LANES, 2 * LANES), BF16)]
    out_specs = [whole(*s.shape) for s in out_shape]
    params = pltpu.CompilerParams(vmem_limit_bytes=VMEM_LIMIT)
    cost = pl.CostEstimate(flops=400_000_000, bytes_accessed=4_000_000, transcendentals=0)
    if b == 0:
        return pl.pallas_call(
            first_kernel,
            grid=(1,),
            in_specs=[whole(MEMBERS, 8, LANES)] + [square] * 4,
            out_specs=out_specs,
            out_shape=out_shape,
            scratch_shapes=[pltpu.VMEM((MEMBERS * 8, LANES), F32)],
            compiler_params=params,
            cost_estimate=cost,
        )(source, slots, weight, observed, noise)
    return pl.pallas_call(
        functools.partial(next_kernel, b),
        grid=(1,),
        in_specs=[pl.BlockSpec(memory_space=pltpu.SMEM), whole(TILES * OWN_MAX, LANES)]
        + [square] * 3
        + [whole(SLOTS, LANES), whole(LANES, LANES)],
        out_specs=out_specs,
        out_shape=out_shape,
        scratch_shapes=[pltpu.VMEM((LANES, LANES), F32)],
        compiler_params=params,
        cost_estimate=cost,
    )(slots, source.reshape(TILES * OWN_MAX, LANES), weight, observed, noise, own, total)


ROWS = 16


def apply_kernel(total_ref, x_ref, out_ref, in_ref, new_ref):
    in_ref[...] = x_ref[...].astype(F32).reshape(MEMBERS * ROWS, LANES)
    total = total_ref[...]
    for v in range(0, ROWS, 2):
        x = jnp.concatenate(
            [in_ref[pl.ds(v + k, MEMBERS, stride=ROWS), :].astype(BF16) for k in range(2)], axis=1
        )
        y = dot(total, jnp.concatenate([x, x], axis=0))
        for k in range(2):
            new_ref[pl.ds(v + k, MEMBERS, stride=ROWS), :] = y[:, k * LANES : (k + 1) * LANES]
    out_ref[...] = new_ref[...].reshape(MEMBERS, ROWS, LANES).astype(BF16)


def apply(total, x):
    block = pl.BlockSpec((MEMBERS, ROWS, LANES), lambda i: (0, i, 0))
    return pl.pallas_call(
        apply_kernel,
        grid=(pl.cdiv(FIELDS, ROWS),),
        in_specs=[pl.BlockSpec((LANES, 2 * LANES), lambda i: (0, 0)), block],
        out_specs=block,
        out_shape=jax.ShapeDtypeStruct((MEMBERS, FIELDS, LANES), BF16),
        scratch_shapes=[pltpu.VMEM((MEMBERS * ROWS, LANES), F32)] * 2,
        compiler_params=pltpu.CompilerParams(vmem_limit_bytes=VMEM_LIMIT),
    )(total, x)


def exchange(x):
    return lax.all_to_all(x, AXES, split_axis=0, concat_axis=0, tiled=False)


def local(
    background_sample,
    measured_reading,
    measurement_noise_variance,
    measurements_in_batch,
    measurement_patch,
    measurement_stack,
    measured_field,
    patch_measurement_roster,
    entry_damping_kind,
):
    owner = measurement_patch.reshape(BATCHES, OBS)
    blocks, message = sort_out(background_sample, owner, measured_field, measurement_stack)
    weight, observed, noise, listed, slots = lists(
        measurements_in_batch, owner, patch_measurement_roster, entry_damping_kind,
        measured_reading, measurement_noise_variance,
    )
    sent, own, total = solve(0, exchange(message), listed, weight, observed, noise, None, None)
    for b in range(1, BATCHES):
        rows = exchange(sent)
        if b == BATCHES - 1:
            rows, blocks = lax.optimization_barrier((rows, blocks))
            (total,) = solve(b, rows, slots, weight, observed, noise, own, total)
        else:
            sent, own, total = solve(b, rows, slots, weight, observed, noise, own, total)
    return apply(total, exchange(blocks))


def solution(mesh):
    in_specs = (
        P(AXES, None, None),
        P(),
        P(),
        P(),
        P(),
        P(),
        P(),
        P(None, AXES, None),
        P(None, AXES, None),
    )
    out_specs = P(None, None, AXES)
    return jax.shard_map(local, mesh=mesh, in_specs=in_specs, out_specs=out_specs, check_vma=False)
```

```python
import functools
import jax
import jax.numpy as jnp
from jax import lax
from jax.experimental import pallas as pl
from jax.experimental.pallas import tpu as pltpu
from jax.sharding import PartitionSpec as P

OWN_MAX = 16
CLASSES = 8
AXES = ("mem", "tile")
BATCHES = 4
OBS = 512
TILES = 128
MEMBERS = 128
LANES = 128
FIELDS = 227
REST = 3
BULK = FIELDS - REST
SENT = BULK + 8
SLOTS = BATCHES * OWN_MAX
GROUP = 16
PAIRS = TILES // 2
GROUPS = TILES // GROUP
VMEM_LIMIT = 16 * 1024 * 1024
HIGHEST = lax.Precision.HIGHEST
F32 = jnp.float32
BF16 = jnp.bfloat16
INVERSE_ROOT = 1.0 / (MEMBERS - 1) ** 0.5


def iota(shape, dim):
    return lax.broadcasted_iota(jnp.int32, shape, dim)


def dot(a, b, precision=None):
    return jnp.dot(a, b, precision=precision, preferred_element_type=F32)


def dot_nt(a, b):
    return lax.dot_general(a, b, (((1,), (1,)), ((), ())), preferred_element_type=F32)


def owner_orders(owner_ref):
    before = jnp.where(iota((LANES, LANES), 0) < iota((LANES, LANES), 1), 1.0, 0.0).astype(BF16)
    count = jnp.concatenate([before, jnp.ones((LANES, LANES), BF16)], axis=0)
    blocks = OBS // LANES
    hots, rows = [], []
    for b in range(BATCHES):
        hot = jnp.where(iota((TILES, OBS), 0) == owner_ref[b], 1.0, 0.0)
        earlier = jnp.zeros((TILES, LANES), F32)
        for k in range(blocks):
            part = hot[:, k * LANES : (k + 1) * LANES]
            rows.append(jnp.concatenate([part, earlier], axis=1).astype(BF16))
            earlier = earlier + part
        hots.append(hot)
    counts = dot(jnp.concatenate(rows, axis=0), count)
    found = []
    for b, hot in enumerate(hots):
        first = b * blocks * TILES
        wide = jnp.concatenate(
            [counts[first + k * TILES : first + (k + 1) * TILES] for k in range(blocks)], axis=1
        )
        found.append((hot, jnp.sum(hot * wide, axis=0, keepdims=True)))
    return found


def pick_kernel(x_ref, owner_ref, field_ref, stack_ref, message_ref,
                in_ref, new_ref, fields_ref, stacks_ref, values_ref, in_sems, out_sems):
    width = GROUP * LANES
    loads = [
        pltpu.make_async_copy(
            x_ref.at[0, :, pl.ds(i * width, width)], in_ref.at[i], in_sems.at[i]
        )
        for i in range(GROUPS)
    ]
    for load in loads:
        load.start()

    slot_of = lax.bitwise_and(iota((LANES, OBS), 0), SLOTS - 1)
    fields = jnp.zeros((TILES, LANES), F32)
    stacks = jnp.zeros((TILES, LANES), F32)
    orders = owner_orders(owner_ref)
    for b, (hot, order) in enumerate(orders):
        slot_hot = slot_of == order.astype(jnp.int32) + b * OWN_MAX
        hot = hot.astype(BF16)
        of_slot = jnp.where(slot_hot, field_ref[b : b + 1, :].astype(F32), 0.0).astype(BF16)
        fields = fields + dot_nt(hot, of_slot)
        of_slot = jnp.where(slot_hot, stack_ref[b : b + 1, :].astype(F32), 0.0).astype(BF16)
        stacks = stacks + dot_nt(hot, of_slot)
    fields_ref[...] = fields
    stacks_ref[...] = stacks

    left = iota((1, LANES), 1) < SLOTS
    column_of = iota((2 * LANES, LANES), 0).astype(F32).astype(BF16)
    field_of = iota((FIELDS, LANES), 0).astype(F32)
    row_of = iota((8, LANES), 0)
    stores = []
    for group in range(GROUPS):
        loads[group].wait()
        block_ref = in_ref.at[group]
        for i in range(GROUP):
            new_ref[group * GROUP + i, 0:BULK, :] = block_ref[0:BULK, i * LANES : (i + 1) * LANES]
        stores.append(
            pltpu.make_async_copy(
                new_ref.at[pl.ds(group * GROUP, GROUP), pl.ds(0, BULK), :],
                message_ref.at[pl.ds(group * GROUP, GROUP), pl.ds(0, BULK), :],
                out_sems.at[group],
            )
        )
        stores[-1].start()
        for i in range(GROUP // 2):
            tile = group * GROUP + 2 * i
            first, second = stacks_ref[tile : tile + 1, :], stacks_ref[tile + 1 : tile + 2, :]
            column = jnp.where(left, first, second + float(LANES)).astype(BF16)
            hot = jnp.where(column_of == column, jnp.ones((), BF16), jnp.zeros((), BF16))
            by_field = dot(block_ref[:, 2 * i * LANES : (2 * i + 2) * LANES], hot)
            first, second = fields_ref[tile : tile + 1, :], fields_ref[tile + 1 : tile + 2, :]
            field = jnp.where(left, first, second)
            values_ref[tile // 2 : tile // 2 + 1, :] = jnp.sum(
                jnp.where(field_of == field, by_field, 0.0), axis=0, keepdims=True
            )

    order = orders[0][1]
    values = values_ref[...]
    turned = values.T.astype(BF16)
    by_slot = jnp.zeros((OWN_MAX, OBS), F32)
    for k in range(2):
        hot = jnp.where(2 * iota((PAIRS, OBS), 0) + k == owner_ref[0], 1.0, 0.0).astype(BF16)
        by_slot = by_slot + dot(turned[k * SLOTS : k * SLOTS + OWN_MAX], hot)
    slot_hot = iota((OWN_MAX, OBS), 0).astype(F32) == order
    first = jnp.sum(jnp.where(slot_hot, by_slot, 0.0), axis=0, keepdims=True)
    base = jnp.zeros((8, LANES), F32)
    for k in range(OBS // LANES):
        base = jnp.where(row_of == k + REST + 1, first[:, k * LANES : (k + 1) * LANES], base)
    for group in range(GROUPS):
        rest = jnp.concatenate(
            [in_ref[group, BULK:, :].astype(F32), jnp.zeros((8 - REST, width), F32)], axis=0
        )
        for i in range(GROUP):
            tile = group * GROUP + i
            end = jnp.where(
                row_of == REST,
                values[tile // 2 : tile // 2 + 1],
                rest[:, i * LANES : (i + 1) * LANES] + base,
            )
            new_ref[tile, BULK:, :] = end.astype(BF16)
    stores.append(
        pltpu.make_async_copy(
            new_ref.at[:, pl.ds(BULK, 8), :],
            message_ref.at[:, pl.ds(BULK, 8), :],
            out_sems.at[GROUPS],
        )
    )
    stores[-1].start()
    for store in stores:
        store.wait()


def pick(x, owner, field, stack):
    vmem = pl.BlockSpec(memory_space=pltpu.VMEM)
    return pl.pallas_call(
        pick_kernel,
        in_specs=[pl.BlockSpec(memory_space=pl.ANY), vmem, vmem, vmem],
        out_specs=pl.BlockSpec(memory_space=pl.ANY),
        out_shape=jax.ShapeDtypeStruct((TILES, SENT, LANES), BF16),
        scratch_shapes=[
            pltpu.VMEM((GROUPS, FIELDS, GROUP * LANES), BF16),
            pltpu.VMEM((TILES, SENT, LANES), BF16),
            pltpu.VMEM((TILES, LANES), F32),
            pltpu.VMEM((TILES, LANES), F32),
            pltpu.VMEM((PAIRS, LANES), F32),
            pltpu.SemaphoreType.DMA((GROUPS,)),
            pltpu.SemaphoreType.DMA((GROUPS + 1,)),
        ],
        compiler_params=pltpu.CompilerParams(vmem_limit_bytes=63_000_000),
    )(x, owner, field, stack)


def column(row):
    eye = iota((LANES, LANES), 0) == iota((LANES, LANES), 1)
    return jnp.broadcast_to(
        jnp.sum(jnp.where(eye, row, 0.0), axis=1, keepdims=True), (LANES, LANES)
    )


def lists_kernel(used_ref, owner_ref, roster_ref, there_ref, kind_ref, reading_ref, variance_ref,
                 weight_ref, observed_ref, noise_ref, listed_ref, near_ref, slot_ref,
                 slot_there_ref):
    core = lax.rem(lax.axis_index("tile"), 2).astype(F32)
    eye = iota((LANES, LANES), 0) == iota((LANES, LANES), 1)
    for b, (_, order) in enumerate(owner_orders(owner_ref)):
        listed = column(roster_ref[b].astype(F32))
        kind = column(kind_ref[b].astype(F32))
        listed_ref[b] = listed.astype(jnp.int32)
        taper = jnp.where(kind > 0.0, (CLASSES + 1 - kind) / CLASSES, 0.0)
        weight_ref[b] = jnp.where(listed < used_ref[b].astype(F32), taper, 0.0)
        owner = owner_ref[b]
        side = lax.bitwise_and(owner, 1).astype(F32)
        slot = lax.shift_right_logical(owner, 1).astype(F32) * OWN_MAX + order

        def hot_of(listed):
            wide = jnp.concatenate([listed] * (OBS // LANES), axis=1)
            return wide == iota((LANES, OBS), 1).astype(F32)

        hot = hot_of(listed)

        def look_up(row, hot=hot):
            return jnp.sum(jnp.where(hot, row, 0.0), axis=1, keepdims=True)

        def slots(hot):
            row = jnp.sum(jnp.where(eye, look_up(slot, hot), 0.0), axis=0, keepdims=True)
            return row.astype(jnp.int32)

        observed_ref[b] = jnp.broadcast_to(look_up(reading_ref[b : b + 1, :]), (LANES, LANES))
        noise_ref[b] = jnp.broadcast_to(look_up(variance_ref[b : b + 1, :]), (LANES, LANES))
        near_ref[b] = jnp.broadcast_to(
            jnp.where(look_up(side) == core, 1.0, 0.0), (LANES, LANES)
        )
        slot_ref[b : b + 1, :] = slots(hot)
        slot_there_ref[b : b + 1, :] = slots(hot_of(column(there_ref[b].astype(F32))))


def lists(used, owner, roster, there, kind, reading, variance):
    vmem = pl.BlockSpec(memory_space=pltpu.VMEM)
    square = jax.ShapeDtypeStruct((BATCHES, LANES, LANES), F32)
    return pl.pallas_call(
        lists_kernel,
        in_specs=[pl.BlockSpec(memory_space=pltpu.SMEM)] + [vmem] * 6,
        out_specs=[vmem] * 7,
        out_shape=[square, square, square, jax.ShapeDtypeStruct(square.shape, jnp.int32), square,
                   jax.ShapeDtypeStruct((BATCHES, LANES), jnp.int32),
                   jax.ShapeDtypeStruct((BATCHES, LANES), jnp.int32)],
        compiler_params=pltpu.CompilerParams(vmem_limit_bytes=VMEM_LIMIT),
    )(used, owner, roster, there, kind, reading, variance)


def transform_of(prior, weight, observed, noise):
    eye = jnp.where(iota((LANES, LANES), 0) == iota((LANES, LANES), 1), 1.0, 0.0)
    mean = jnp.sum(prior, axis=1, keepdims=True) * (1.0 / MEMBERS)
    scaled = weight * (prior - mean) * INVERSE_ROOT
    inverse_noise = 1.0 / noise
    right = jnp.concatenate(
        [scaled * inverse_noise, weight * (observed - mean) * inverse_noise], axis=1
    )
    both = dot(scaled.T, right, HIGHEST)
    matrix = both[:, :LANES] + eye
    pull = both[:, LANES:]
    bound = jnp.max(jnp.sum(jnp.abs(matrix), axis=0, keepdims=True)) * 1.00001
    scale = 2.0 / (1.0 + bound)
    rho = (bound - 1.0) / (bound + 1.0)

    def unfinished(carry):
        return carry[0] > 3e-4

    def square(carry):
        rho, x, e = carry
        gain = 2.0 / (2.0 - rho * rho)
        products = dot(jnp.concatenate([x, e], axis=0), e, HIGHEST)
        x = gain * (x + products[:LANES])
        e = gain * products[LANES:] + (1.0 - gain) * eye
        return rho * rho / (2.0 - rho * rho), x, e

    _, inverse, _ = lax.while_loop(unfinished, square, (rho, scale * eye, eye - scale * matrix))

    def refine(_, x):
        return x + dot(x, eye - dot(matrix, x, HIGHEST), HIGHEST)

    inverse = lax.fori_loop(0, jnp.where(bound > 200.0, 2, 1), refine, inverse)
    return 0.5 * (eye + inverse) + dot(inverse, pull, HIGHEST) * INVERSE_ROOT


def first_kernel(message_ref, listed_ref, weight_ref, observed_ref, noise_ref,
                 sent_ref, own_ref, total_ref, scratch_ref):
    odd = lax.rem(lax.axis_index("tile"), 2) == 1
    scratch_ref[...] = message_ref[:, 0:8, :].astype(F32).reshape(MEMBERS * 8, LANES)
    listed = listed_ref[0]
    prior = jnp.zeros((LANES, MEMBERS), F32)
    for k in range(OBS // LANES):
        values = scratch_ref[pl.ds(REST + 1 + k, MEMBERS, stride=8), :].astype(BF16)
        hot = jnp.where(listed == iota((LANES, LANES), 1) + k * LANES, 1.0, 0.0).astype(BF16)
        prior = prior + dot_nt(hot, values)
    pair = scratch_ref[pl.ds(REST, MEMBERS, stride=8), :].T
    own = jnp.where(odd, pair[SLOTS:], pair[:SLOTS])
    transform = transform_of(prior, weight_ref[0], observed_ref[0], noise_ref[0])
    own = dot(own, transform, HIGHEST)
    own_ref[...] = own
    total_ref[...] = transform
    sent_ref[...] = jnp.broadcast_to(own[OWN_MAX : 2 * OWN_MAX][None], (PAIRS, OWN_MAX, LANES))


def next_kernel(b, near_ref, far_ref, side_ref, weight_ref, observed_ref, noise_ref, own_ref,
                total_ref, *outs):
    prior = jnp.where(side_ref[0] > 0.0, near_ref[...], far_ref[...])
    transform = transform_of(prior, weight_ref[0], observed_ref[0], noise_ref[0])
    if b < BATCHES - 1:
        sent_ref, own_out_ref, total_out_ref = outs
        own = dot(own_ref[...], transform, HIGHEST)
        own_out_ref[...] = own
        total_out_ref[...] = dot(total_ref[...], transform, HIGHEST)
        sent = own[(b + 1) * OWN_MAX : (b + 2) * OWN_MAX]
        sent_ref[...] = jnp.broadcast_to(sent[None], (PAIRS, OWN_MAX, LANES))
    else:
        total = dot(total_ref[...], transform, HIGHEST).T
        high = total.astype(BF16)
        outs[0][:, :LANES] = high
        outs[0][:, LANES:] = (total - high.astype(F32)).astype(BF16)


def whole(*shape):
    return pl.BlockSpec(shape, lambda i: (0,) * len(shape))


def solve(b, near, far, lists_of, own=None, total=None):
    weight, observed, noise, listed, side = lists_of[:5]
    square = pl.BlockSpec((1, LANES, LANES), lambda i: (b, 0, 0))
    sent = jax.ShapeDtypeStruct((PAIRS, OWN_MAX, LANES), F32)
    owned = jax.ShapeDtypeStruct((SLOTS, LANES), F32)
    full = jax.ShapeDtypeStruct((LANES, LANES), F32)
    if b < BATCHES - 1:
        out_shape = [sent, owned, full]
    else:
        out_shape = [jax.ShapeDtypeStruct((LANES, 2 * LANES), BF16)]
    out_specs = [whole(*s.shape) for s in out_shape]
    params = pltpu.CompilerParams(vmem_limit_bytes=VMEM_LIMIT)
    cost = pl.CostEstimate(flops=400_000_000, bytes_accessed=4_000_000, transcendentals=0)
    if b == 0:
        return pl.pallas_call(
            first_kernel,
            grid=(1,),
            in_specs=[pl.BlockSpec((MEMBERS, 16, LANES), lambda i: (0, BULK // 16, 0))] + [square] * 4,
            out_specs=out_specs,
            out_shape=out_shape,
            scratch_shapes=[pltpu.VMEM((MEMBERS * 8, LANES), F32)],
            compiler_params=params,
            cost_estimate=cost,
        )(near, listed, weight, observed, noise)
    return pl.pallas_call(
        functools.partial(next_kernel, b),
        grid=(1,),
        in_specs=[whole(LANES, LANES)] * 2
        + [square] * 4
        + [whole(SLOTS, LANES), whole(LANES, LANES)],
        out_specs=out_specs,
        out_shape=out_shape,
        compiler_params=params,
        cost_estimate=cost,
    )(near, far, side, weight, observed, noise, own, total)


def select_kernel(b, slot_ref, rows_ref, out_ref):
    for slot in range(LANES):
        out_ref[slot : slot + 1, :] = rows_ref[pl.ds(slot_ref[b, slot], 1), :]


def select(b, slots, rows):
    return pl.pallas_call(
        functools.partial(select_kernel, b),
        grid=(1,),
        in_specs=[pl.BlockSpec(memory_space=pltpu.SMEM), whole(PAIRS * OWN_MAX, LANES)],
        out_specs=whole(LANES, LANES),
        out_shape=jax.ShapeDtypeStruct((LANES, LANES), F32),
        compiler_params=pltpu.CompilerParams(vmem_limit_bytes=VMEM_LIMIT),
        cost_estimate=pl.CostEstimate(flops=0, bytes_accessed=1_000_000, transcendentals=0),
    )(slots, rows)


ROWS = 32
CHUNKS = BULK // ROWS


def turn_kernel(end_ref, x_ref, out_ref, in_ref, flat_ref, sems):
    loads = [
        pltpu.make_async_copy(x_ref.at[:, pl.ds(i * ROWS, ROWS), :], in_ref.at[i], sems.at[i])
        for i in range(CHUNKS)
    ]
    for load in loads:
        load.start()
    flat_ref[:, 0:8, :] = end_ref[:, 0:8, :].astype(F32)
    rows_ref = flat_ref.reshape(MEMBERS * (ROWS + 8), LANES)

    def row(v):
        return rows_ref[pl.ds(v, MEMBERS, stride=ROWS + 8), :].astype(BF16)

    for k in range(REST):
        out_ref[BULK + k] = row(k)
    for k in range(FIELDS, SENT):
        out_ref[k] = jnp.zeros((MEMBERS, LANES), BF16)
    for i in range(CHUNKS):
        loads[i].wait()
        flat_ref[:, 0:ROWS, :] = in_ref[i].astype(F32)
        for v in range(ROWS):
            out_ref[i * ROWS + v] = row(v)


def turn(x):
    return pl.pallas_call(
        turn_kernel,
        in_specs=[
            pl.BlockSpec((MEMBERS, 16, LANES), lambda i: (0, BULK // 16, 0)),
            pl.BlockSpec(memory_space=pl.ANY),
        ],
        grid=(1,),
        out_specs=whole(SENT, MEMBERS, LANES),
        out_shape=jax.ShapeDtypeStruct((SENT, MEMBERS, LANES), BF16),
        scratch_shapes=[
            pltpu.VMEM((CHUNKS, MEMBERS, ROWS, LANES), BF16),
            pltpu.VMEM((MEMBERS, ROWS + 8, LANES), F32),
            pltpu.SemaphoreType.DMA((CHUNKS,)),
        ],
        compiler_params=pltpu.CompilerParams(vmem_limit_bytes=30 * 1024 * 1024),
        cost_estimate=pl.CostEstimate(flops=0, bytes_accessed=15_000_000, transcendentals=0),
    )(x, x)


STEP = SENT // 4


def apply_kernel(total_ref, x_ref, out_ref):
    total = total_ref[...]
    first = pl.program_id(0) * STEP
    for v in range(0, STEP, 2):
        x = jnp.concatenate([x_ref[first + v], x_ref[first + v + 1]], axis=1)
        y = dot(total, jnp.concatenate([x, x], axis=0)).astype(BF16)
        for k in range(2):
            out_ref[v + k] = y[:, k * LANES : (k + 1) * LANES]


def apply(total, x):
    return pl.pallas_call(
        apply_kernel,
        grid=(SENT // STEP,),
        in_specs=[whole(LANES, 2 * LANES), pl.BlockSpec(memory_space=pltpu.VMEM)],
        out_specs=pl.BlockSpec((STEP, MEMBERS, LANES), lambda i: (i, 0, 0)),
        out_shape=jax.ShapeDtypeStruct((FIELDS, MEMBERS, LANES), BF16),
        compiler_params=pltpu.CompilerParams(vmem_limit_bytes=30 * 1024 * 1024),
    )(total, x)


def exchange(x, groups=None):
    return lax.all_to_all(x, AXES, split_axis=0, concat_axis=0, axis_index_groups=groups)


def to_chips(x):
    return exchange(x, [list(range(core, TILES, 2)) for core in range(2)])


def swap(x):
    size = lax.axis_size("tile")
    return lax.ppermute(x, "tile", [(i, i ^ 1) for i in range(size)])


def local(
    background_sample,
    measured_reading,
    measurement_noise_variance,
    measurements_in_batch,
    measurement_patch,
    measurement_stack,
    measured_field,
    patch_measurement_roster,
    entry_damping_kind,
):
    owner = measurement_patch.reshape(BATCHES, 1, OBS)
    roster_there = swap(patch_measurement_roster)
    message = pick(background_sample, owner, measured_field, measurement_stack)
    message, used = lax.optimization_barrier((message, measurements_in_batch))
    lists_of = lists(
        used, owner, patch_measurement_roster, roster_there, entry_damping_kind,
        measured_reading, measurement_noise_variance,
    )
    fields, lists_of = lax.optimization_barrier((exchange(message), lists_of))
    slots, slots_there = lists_of[-2:]
    sent, own, total = solve(0, fields, None, lists_of)
    sent, fields_later = lax.optimization_barrier((sent, fields))
    for b in range(1, BATCHES):
        rows = to_chips(sent).reshape(PAIRS * OWN_MAX, LANES)
        if b == 1:
            rows, turned = lax.optimization_barrier((rows, turn(fields_later)))
        far = swap(select(b, slots_there, rows))
        near = select(b, slots, rows)
        if b == BATCHES - 1:
            (total,) = solve(b, near, far, lists_of, own, total)
        else:
            sent, own, total = solve(b, near, far, lists_of, own, total)
    return apply(total, turned).transpose(1, 0, 2)


def solution(mesh):
    in_specs = (
        P(AXES, None, None),
        P(),
        P(),
        P(),
        P(),
        P(),
        P(),
        P(None, AXES, None),
        P(None, AXES, None),
    )
    out_specs = P(None, None, AXES)
    return jax.shard_map(local, mesh=mesh, in_specs=in_specs, out_specs=out_specs, check_vma=False)
```

```python
import functools
import jax
import jax.numpy as jnp
from jax import lax
from jax.experimental import pallas as pl
from jax.experimental.pallas import tpu as pltpu
from jax.sharding import PartitionSpec as P

OWN_MAX = 16
CLASSES = 8
AXES = ("mem", "tile")
BATCHES = 4
OBS = 512
TILES = 128
MEMBERS = 128
LANES = 128
FIELDS = 227
REST = 3
BULK = FIELDS - REST
SENT = BULK + 8
SLOTS = BATCHES * OWN_MAX
GROUP = 16
PAIRS = TILES // 2
GROUPS = TILES // GROUP
VMEM_LIMIT = 16 * 1024 * 1024
HIGHEST = lax.Precision.HIGHEST
F32 = jnp.float32
FINEST = 0.25
CODES_PER_OCTAVE = 1326.0
BF16 = jnp.bfloat16
INVERSE_ROOT = 1.0 / (MEMBERS - 1) ** 0.5


def iota(shape, dim):
    return lax.broadcasted_iota(jnp.int32, shape, dim)


def dot(a, b, precision=None):
    return jnp.dot(a, b, precision=precision, preferred_element_type=F32)


def dot_nt(a, b):
    return lax.dot_general(a, b, (((1,), (1,)), ((), ())), preferred_element_type=F32)


def owner_orders(owner_ref):
    before = jnp.where(iota((LANES, LANES), 0) < iota((LANES, LANES), 1), 1.0, 0.0).astype(BF16)
    count = jnp.concatenate([before, jnp.ones((LANES, LANES), BF16)], axis=0)
    blocks = OBS // LANES
    hots, rows = [], []
    for b in range(BATCHES):
        hot = jnp.where(iota((TILES, OBS), 0) == owner_ref[b], 1.0, 0.0)
        earlier = jnp.zeros((TILES, LANES), F32)
        for k in range(blocks):
            part = hot[:, k * LANES : (k + 1) * LANES]
            rows.append(jnp.concatenate([part, earlier], axis=1).astype(BF16))
            earlier = earlier + part
        hots.append(hot)
    counts = dot(jnp.concatenate(rows, axis=0), count)
    found = []
    for b, hot in enumerate(hots):
        first = b * blocks * TILES
        wide = jnp.concatenate(
            [counts[first + k * TILES : first + (k + 1) * TILES] for k in range(blocks)], axis=1
        )
        found.append((hot, jnp.sum(hot * wide, axis=0, keepdims=True)))
    return found


def pick_kernel(x_ref, owner_ref, field_ref, stack_ref, message_ref,
                in_ref, new_ref, fields_ref, stacks_ref, values_ref, in_sems, out_sems):
    width = GROUP * LANES
    loads = [
        pltpu.make_async_copy(
            x_ref.at[0, :, pl.ds(i * width, width)], in_ref.at[i], in_sems.at[i]
        )
        for i in range(GROUPS)
    ]
    for load in loads:
        load.start()

    slot_of = lax.bitwise_and(iota((LANES, OBS), 0), SLOTS - 1)
    fields = jnp.zeros((TILES, LANES), F32)
    stacks = jnp.zeros((TILES, LANES), F32)
    orders = owner_orders(owner_ref)
    for b, (hot, order) in enumerate(orders):
        slot_hot = slot_of == order.astype(jnp.int32) + b * OWN_MAX
        hot = hot.astype(BF16)
        of_slot = jnp.where(slot_hot, field_ref[b : b + 1, :].astype(F32), 0.0).astype(BF16)
        fields = fields + dot_nt(hot, of_slot)
        of_slot = jnp.where(slot_hot, stack_ref[b : b + 1, :].astype(F32), 0.0).astype(BF16)
        stacks = stacks + dot_nt(hot, of_slot)
    fields_ref[...] = fields
    stacks_ref[...] = stacks

    left = iota((1, LANES), 1) < SLOTS
    column_of = iota((2 * LANES, LANES), 0).astype(F32).astype(BF16)
    field_of = iota((FIELDS, LANES), 0).astype(F32)
    row_of = iota((8, LANES), 0)
    stores = []
    for group in range(GROUPS):
        loads[group].wait()
        block_ref = in_ref.at[group]
        for i in range(GROUP):
            new_ref[group * GROUP + i, 0:BULK, :] = block_ref[0:BULK, i * LANES : (i + 1) * LANES]
        stores.append(
            pltpu.make_async_copy(
                new_ref.at[pl.ds(group * GROUP, GROUP), pl.ds(0, BULK), :],
                message_ref.at[pl.ds(group * GROUP, GROUP), pl.ds(0, BULK), :],
                out_sems.at[group],
            )
        )
        stores[-1].start()
        for i in range(GROUP // 2):
            tile = group * GROUP + 2 * i
            first, second = stacks_ref[tile : tile + 1, :], stacks_ref[tile + 1 : tile + 2, :]
            column = jnp.where(left, first, second + float(LANES)).astype(BF16)
            hot = jnp.where(column_of == column, jnp.ones((), BF16), jnp.zeros((), BF16))
            by_field = dot(block_ref[:, 2 * i * LANES : (2 * i + 2) * LANES], hot)
            first, second = fields_ref[tile : tile + 1, :], fields_ref[tile + 1 : tile + 2, :]
            field = jnp.where(left, first, second)
            values_ref[tile // 2 : tile // 2 + 1, :] = jnp.sum(
                jnp.where(field_of == field, by_field, 0.0), axis=0, keepdims=True
            )

    order = orders[0][1]
    values = values_ref[...]
    turned = values.T.astype(BF16)
    by_slot = jnp.zeros((OWN_MAX, OBS), F32)
    for k in range(2):
        hot = jnp.where(2 * iota((PAIRS, OBS), 0) + k == owner_ref[0], 1.0, 0.0).astype(BF16)
        by_slot = by_slot + dot(turned[k * SLOTS : k * SLOTS + OWN_MAX], hot)
    slot_hot = iota((OWN_MAX, OBS), 0).astype(F32) == order
    first = jnp.sum(jnp.where(slot_hot, by_slot, 0.0), axis=0, keepdims=True)
    base = jnp.zeros((8, LANES), F32)
    for k in range(OBS // LANES):
        base = jnp.where(row_of == k + REST + 1, first[:, k * LANES : (k + 1) * LANES], base)
    for group in range(GROUPS):
        rest = jnp.concatenate(
            [in_ref[group, BULK:, :].astype(F32), jnp.zeros((8 - REST, width), F32)], axis=0
        )
        for i in range(GROUP):
            tile = group * GROUP + i
            end = jnp.where(
                row_of == REST,
                values[tile // 2 : tile // 2 + 1],
                rest[:, i * LANES : (i + 1) * LANES] + base,
            )
            new_ref[tile, BULK:, :] = end.astype(BF16)
    stores.append(
        pltpu.make_async_copy(
            new_ref.at[:, pl.ds(BULK, 8), :],
            message_ref.at[:, pl.ds(BULK, 8), :],
            out_sems.at[GROUPS],
        )
    )
    stores[-1].start()
    for store in stores:
        store.wait()


def pick(x, owner, field, stack):
    vmem = pl.BlockSpec(memory_space=pltpu.VMEM)
    return pl.pallas_call(
        pick_kernel,
        in_specs=[pl.BlockSpec(memory_space=pl.ANY), vmem, vmem, vmem],
        out_specs=pl.BlockSpec(memory_space=pl.ANY),
        out_shape=jax.ShapeDtypeStruct((TILES, SENT, LANES), BF16),
        scratch_shapes=[
            pltpu.VMEM((GROUPS, FIELDS, GROUP * LANES), BF16),
            pltpu.VMEM((TILES, SENT, LANES), BF16),
            pltpu.VMEM((TILES, LANES), F32),
            pltpu.VMEM((TILES, LANES), F32),
            pltpu.VMEM((PAIRS, LANES), F32),
            pltpu.SemaphoreType.DMA((GROUPS,)),
            pltpu.SemaphoreType.DMA((GROUPS + 1,)),
        ],
        compiler_params=pltpu.CompilerParams(vmem_limit_bytes=63_000_000),
    )(x, owner, field, stack)


def column(row):
    eye = iota((LANES, LANES), 0) == iota((LANES, LANES), 1)
    return jnp.broadcast_to(
        jnp.sum(jnp.where(eye, row, 0.0), axis=1, keepdims=True), (LANES, LANES)
    )


def lists_kernel(used_ref, owner_ref, roster_ref, there_ref, kind_ref, reading_ref, variance_ref,
                 weight_ref, observed_ref, noise_ref, listed_ref, near_ref, slot_ref,
                 slot_there_ref):
    core = lax.rem(lax.axis_index("tile"), 2).astype(F32)
    eye = iota((LANES, LANES), 0) == iota((LANES, LANES), 1)
    for b, (_, order) in enumerate(owner_orders(owner_ref)):
        listed = column(roster_ref[b].astype(F32))
        kind = column(kind_ref[b].astype(F32))
        listed_ref[b] = listed.astype(jnp.int32)
        taper = jnp.where(kind > 0.0, (CLASSES + 1 - kind) / CLASSES, 0.0)
        weight_ref[b] = jnp.where(listed < used_ref[b].astype(F32), taper, 0.0)
        owner = owner_ref[b]
        side = lax.bitwise_and(owner, 1).astype(F32)
        slot = lax.shift_right_logical(owner, 1).astype(F32) * OWN_MAX + order

        def hot_of(listed):
            wide = jnp.concatenate([listed] * (OBS // LANES), axis=1)
            return wide == iota((LANES, OBS), 1).astype(F32)

        hot = hot_of(listed)

        def look_up(row, hot=hot):
            return jnp.sum(jnp.where(hot, row, 0.0), axis=1, keepdims=True)

        def slots(hot):
            row = jnp.sum(jnp.where(eye, look_up(slot, hot), 0.0), axis=0, keepdims=True)
            return row.astype(jnp.int32)

        observed_ref[b] = jnp.broadcast_to(look_up(reading_ref[b : b + 1, :]), (LANES, LANES))
        noise_ref[b] = jnp.broadcast_to(look_up(variance_ref[b : b + 1, :]), (LANES, LANES))
        near_ref[b] = jnp.broadcast_to(
            jnp.where(look_up(side) == core, 1.0, 0.0), (LANES, LANES)
        )
        slot_ref[b : b + 1, :] = slots(hot)
        slot_there_ref[b : b + 1, :] = slots(hot_of(column(there_ref[b].astype(F32))))


def lists(used, owner, roster, there, kind, reading, variance):
    vmem = pl.BlockSpec(memory_space=pltpu.VMEM)
    square = jax.ShapeDtypeStruct((BATCHES, LANES, LANES), F32)
    return pl.pallas_call(
        lists_kernel,
        in_specs=[pl.BlockSpec(memory_space=pltpu.SMEM)] + [vmem] * 6,
        out_specs=[vmem] * 7,
        out_shape=[square, square, square, jax.ShapeDtypeStruct(square.shape, jnp.int32), square,
                   jax.ShapeDtypeStruct((BATCHES, LANES), jnp.int32),
                   jax.ShapeDtypeStruct((BATCHES, LANES), jnp.int32)],
        compiler_params=pltpu.CompilerParams(vmem_limit_bytes=VMEM_LIMIT),
    )(used, owner, roster, there, kind, reading, variance)


def coded(x):
    size = CODES_PER_OCTAVE * jnp.log2(1.0 + jnp.abs(x) * (1.0 / FINEST))
    return jnp.round(jnp.where(x < 0.0, -size, size)).astype(jnp.int32).astype(jnp.int16)


def decoded(code):
    size = jnp.exp2(jnp.abs(code) * (1.0 / CODES_PER_OCTAVE)) - 1.0
    return jnp.where(code < 0.0, -FINEST, FINEST) * size


def transform_of(prior, weight, observed, noise):
    eye = jnp.where(iota((LANES, LANES), 0) == iota((LANES, LANES), 1), 1.0, 0.0)
    mean = jnp.sum(prior, axis=1, keepdims=True) * (1.0 / MEMBERS)
    scaled = weight * (prior - mean) * INVERSE_ROOT
    inverse_noise = 1.0 / noise
    right = jnp.concatenate(
        [scaled * inverse_noise, weight * (observed - mean) * inverse_noise], axis=1
    )
    both = dot(scaled.T, right, HIGHEST)
    matrix = both[:, :LANES] + eye
    pull = both[:, LANES:]
    bound = jnp.max(jnp.sum(jnp.abs(matrix), axis=0, keepdims=True)) * 1.00001
    scale = 2.0 / (1.0 + bound)
    rho = (bound - 1.0) / (bound + 1.0)

    def unfinished(carry):
        return carry[0] > 3e-4

    def square(carry):
        rho, x, e = carry
        gain = 2.0 / (2.0 - rho * rho)
        products = dot(jnp.concatenate([x, e], axis=0), e, lax.Precision.HIGH)
        x = gain * (x + products[:LANES])
        e = gain * products[LANES:] + (1.0 - gain) * eye
        return rho * rho / (2.0 - rho * rho), x, e

    _, inverse, _ = lax.while_loop(unfinished, square, (rho, scale * eye, eye - scale * matrix))

    def refine(_, x):
        return x + dot(x, eye - dot(matrix, x, HIGHEST), HIGHEST)

    inverse = lax.fori_loop(0, jnp.where(bound > 200.0, 2, 1), refine, inverse)
    return 0.5 * (eye + inverse) + dot(inverse, pull, HIGHEST) * INVERSE_ROOT


def first_kernel(message_ref, listed_ref, weight_ref, observed_ref, noise_ref,
                 sent_ref, own_ref, total_ref, scratch_ref):
    odd = lax.rem(lax.axis_index("tile"), 2) == 1
    scratch_ref[...] = message_ref[:, 0:8, :].astype(F32).reshape(MEMBERS * 8, LANES)
    listed = listed_ref[0]
    values = jnp.concatenate(
        [
            scratch_ref[pl.ds(REST + 1 + k, MEMBERS, stride=8), :].astype(BF16)
            for k in range(OBS // LANES)
        ],
        axis=1,
    )
    hot = jnp.concatenate(
        [
            jnp.where(listed == iota((LANES, LANES), 1) + k * LANES, 1.0, 0.0).astype(BF16)
            for k in range(OBS // LANES)
        ],
        axis=1,
    )
    prior = dot_nt(hot, values)
    pair = scratch_ref[pl.ds(REST, MEMBERS, stride=8), :].T
    own = jnp.where(odd, pair[SLOTS:], pair[:SLOTS])
    transform = transform_of(prior, weight_ref[0], observed_ref[0], noise_ref[0])
    own = dot(own, transform, HIGHEST)
    own_ref[...] = own
    total_ref[...] = transform
    sent_ref[...] = jnp.broadcast_to(
        coded(own[OWN_MAX : 2 * OWN_MAX])[None], (PAIRS, OWN_MAX, LANES)
    )


def next_kernel(b, near_ref, far_ref, side_ref, weight_ref, observed_ref, noise_ref, own_ref,
                total_ref, *outs):
    near = near_ref[...].astype(jnp.int32).astype(F32)
    far = far_ref[...].astype(jnp.int32).astype(F32)
    prior = decoded(jnp.where(side_ref[0] > 0.0, near, far))
    transform = transform_of(prior, weight_ref[0], observed_ref[0], noise_ref[0])
    if b < BATCHES - 1:
        sent_ref, own_out_ref, total_out_ref = outs
        own = dot(own_ref[...], transform, HIGHEST)
        own_out_ref[...] = own
        total_out_ref[...] = dot(total_ref[...], transform, HIGHEST)
        sent = own[(b + 1) * OWN_MAX : (b + 2) * OWN_MAX]
        sent_ref[...] = jnp.broadcast_to(coded(sent)[None], (PAIRS, OWN_MAX, LANES))
    else:
        total = dot(total_ref[...], transform, HIGHEST).T
        high = total.astype(BF16)
        outs[0][:, :LANES] = high
        outs[0][:, LANES:] = (total - high.astype(F32)).astype(BF16)


def whole(*shape):
    return pl.BlockSpec(shape, lambda i: (0,) * len(shape))


def solve(b, near, far, lists_of, own=None, total=None):
    weight, observed, noise, listed, side = lists_of[:5]
    square = pl.BlockSpec((1, LANES, LANES), lambda i: (b, 0, 0))
    sent = jax.ShapeDtypeStruct((PAIRS, OWN_MAX, LANES), jnp.int16)
    owned = jax.ShapeDtypeStruct((SLOTS, LANES), F32)
    full = jax.ShapeDtypeStruct((LANES, LANES), F32)
    if b < BATCHES - 1:
        out_shape = [sent, owned, full]
    else:
        out_shape = [jax.ShapeDtypeStruct((LANES, 2 * LANES), BF16)]
    out_specs = [whole(*s.shape) for s in out_shape]
    params = pltpu.CompilerParams(vmem_limit_bytes=VMEM_LIMIT)
    cost = pl.CostEstimate(flops=400_000_000, bytes_accessed=4_000_000, transcendentals=0)
    if b == 0:
        return pl.pallas_call(
            first_kernel,
            grid=(1,),
            in_specs=[pl.BlockSpec((MEMBERS, 16, LANES), lambda i: (0, BULK // 16, 0))] + [square] * 4,
            out_specs=out_specs,
            out_shape=out_shape,
            scratch_shapes=[pltpu.VMEM((MEMBERS * 8, LANES), F32)],
            compiler_params=params,
            cost_estimate=cost,
        )(near, listed, weight, observed, noise)
    return pl.pallas_call(
        functools.partial(next_kernel, b),
        grid=(1,),
        in_specs=[whole(LANES, LANES)] * 2
        + [square] * 4
        + [whole(SLOTS, LANES), whole(LANES, LANES)],
        out_specs=out_specs,
        out_shape=out_shape,
        compiler_params=params,
        cost_estimate=cost,
    )(near, far, side, weight, observed, noise, own, total)


def select_kernel(b, slot_ref, rows_ref, out_ref, wide_ref, found_ref):
    wide_ref[...] = rows_ref[...].astype(jnp.int32)
    for slot in range(LANES):
        found_ref[slot : slot + 1, :] = wide_ref[pl.ds(slot_ref[b, slot], 1), :]
    out_ref[...] = found_ref[...].astype(jnp.int16)


def select(b, slots, rows):
    return pl.pallas_call(
        functools.partial(select_kernel, b),
        grid=(1,),
        in_specs=[pl.BlockSpec(memory_space=pltpu.SMEM), whole(PAIRS * OWN_MAX, LANES)],
        out_specs=whole(LANES, LANES),
        out_shape=jax.ShapeDtypeStruct((LANES, LANES), jnp.int16),
        scratch_shapes=[
            pltpu.VMEM((PAIRS * OWN_MAX, LANES), jnp.int32),
            pltpu.VMEM((LANES, LANES), jnp.int32),
        ],
        compiler_params=pltpu.CompilerParams(vmem_limit_bytes=VMEM_LIMIT),
        cost_estimate=pl.CostEstimate(flops=0, bytes_accessed=1_000_000, transcendentals=0),
    )(slots, rows)


ROWS = 32
CHUNKS = BULK // ROWS


def apply_kernel(total_ref, x_ref, out_ref, in_ref, end_ref, new_ref, flat_ref, in_sems, out_sems):
    loads = [
        pltpu.make_async_copy(x_ref.at[:, pl.ds(i * ROWS, ROWS), :], in_ref.at[i], in_sems.at[i])
        for i in range(CHUNKS)
    ]
    loads.append(
        pltpu.make_async_copy(x_ref.at[:, pl.ds(BULK, 8), :], end_ref, in_sems.at[CHUNKS])
    )
    for load in loads:
        load.start()
    total = total_ref[...]
    rows_ref = flat_ref.reshape(MEMBERS * (ROWS + 8), LANES)

    def row(v):
        return rows_ref[pl.ds(v, MEMBERS, stride=ROWS + 8), :].astype(BF16)

    def transformed(x):
        return dot(total, jnp.concatenate([x, x], axis=0)).astype(BF16)

    stores = []
    for i in range(CHUNKS + 1):
        loads[i].wait()
        number = ROWS if i < CHUNKS else REST
        if i < CHUNKS:
            flat_ref[:, 0:ROWS, :] = in_ref[i].astype(F32)
        else:
            flat_ref[:, 0:8, :] = end_ref[...].astype(F32)
        for v in range(0, number, 2):
            y = transformed(jnp.concatenate([row(v), row(v + 1)], axis=1))
            for k in range(min(2, number - v)):
                new_ref[i * ROWS + v + k] = y[:, k * LANES : (k + 1) * LANES]
        places = pl.ds(i * ROWS, number)
        stores.append(
            pltpu.make_async_copy(new_ref.at[places], out_ref.at[places], out_sems.at[i])
        )
        stores[-1].start()
    for store in stores:
        store.wait()


def apply(total, x):
    return pl.pallas_call(
        apply_kernel,
        in_specs=[
            pl.BlockSpec(memory_space=pltpu.VMEM),
            pl.BlockSpec(memory_space=pl.ANY),
        ],
        out_specs=pl.BlockSpec(memory_space=pl.ANY),
        out_shape=jax.ShapeDtypeStruct((FIELDS, MEMBERS, LANES), BF16),
        scratch_shapes=[
            pltpu.VMEM((CHUNKS, MEMBERS, ROWS, LANES), BF16),
            pltpu.VMEM((MEMBERS, 8, LANES), BF16),
            pltpu.VMEM((FIELDS, MEMBERS, LANES), BF16),
            pltpu.VMEM((MEMBERS, ROWS + 8, LANES), F32),
            pltpu.SemaphoreType.DMA((CHUNKS + 1,)),
            pltpu.SemaphoreType.DMA((CHUNKS + 1,)),
        ],
        compiler_params=pltpu.CompilerParams(vmem_limit_bytes=60_000_000),
    )(total, x)


def exchange(x, groups=None):
    return lax.all_to_all(x, AXES, split_axis=0, concat_axis=0, axis_index_groups=groups)


def to_chips(x):
    return exchange(x, [list(range(core, TILES, 2)) for core in range(2)])


def swap(x):
    size = lax.axis_size("tile")
    return lax.ppermute(x, "tile", [(i, i ^ 1) for i in range(size)])


def local(
    background_sample,
    measured_reading,
    measurement_noise_variance,
    measurements_in_batch,
    measurement_patch,
    measurement_stack,
    measured_field,
    patch_measurement_roster,
    entry_damping_kind,
):
    owner = measurement_patch.reshape(BATCHES, 1, OBS)
    roster_there = swap(patch_measurement_roster)
    message = pick(background_sample, owner, measured_field, measurement_stack)
    message, used = lax.optimization_barrier((message, measurements_in_batch))
    lists_of = lists(
        used, owner, patch_measurement_roster, roster_there, entry_damping_kind,
        measured_reading, measurement_noise_variance,
    )
    fields, lists_of = lax.optimization_barrier((exchange(message), lists_of))
    slots, slots_there = lists_of[-2:]
    sent, own, total = solve(0, fields, None, lists_of)
    for b in range(1, BATCHES):
        rows = to_chips(sent).reshape(PAIRS * OWN_MAX, LANES)
        far = swap(select(b, slots_there, rows))
        near = select(b, slots, rows)
        if b == BATCHES - 1:
            (total,) = solve(b, near, far, lists_of, own, total)
        else:
            sent, own, total = solve(b, near, far, lists_of, own, total)
    return apply(total, fields).transpose(1, 0, 2)


def solution(mesh):
    in_specs = (
        P(AXES, None, None),
        P(),
        P(),
        P(),
        P(),
        P(),
        P(),
        P(None, AXES, None),
        P(None, AXES, None),
    )
    out_specs = P(None, None, AXES)
    return jax.shard_map(local, mesh=mesh, in_specs=in_specs, out_specs=out_specs, check_vma=False)
```

```python
import functools
import jax
import jax.numpy as jnp
from jax import lax
from jax.experimental import pallas as pl
from jax.experimental.pallas import tpu as pltpu
from jax.sharding import PartitionSpec as P

OWN_MAX = 16
CLASSES = 8
AXES = ("mem", "tile")
BATCHES = 4
OBS = 512
TILES = 128
MEMBERS = 128
LANES = 128
FIELDS = 227
REST = 3
BULK = FIELDS - REST
SENT = BULK + 8
SLOTS = BATCHES * OWN_MAX
GROUP = 16
PAIRS = TILES // 2
GROUPS = TILES // GROUP
VMEM_LIMIT = 16 * 1024 * 1024
HIGHEST = lax.Precision.HIGHEST
F32 = jnp.float32
FINEST = 0.25
CODES_PER_OCTAVE = 1326.0
BF16 = jnp.bfloat16
INVERSE_ROOT = 1.0 / (MEMBERS - 1) ** 0.5


def iota(shape, dim):
    return lax.broadcasted_iota(jnp.int32, shape, dim)


def dot(a, b, precision=None):
    return jnp.dot(a, b, precision=precision, preferred_element_type=F32)


def dot_nt(a, b):
    return lax.dot_general(a, b, (((1,), (1,)), ((), ())), preferred_element_type=F32)


def owner_orders(owner_ref):
    before = jnp.where(iota((LANES, LANES), 0) < iota((LANES, LANES), 1), 1.0, 0.0).astype(BF16)
    count = jnp.concatenate([before, jnp.ones((LANES, LANES), BF16)], axis=0)
    blocks = OBS // LANES
    hots, rows = [], []
    for b in range(BATCHES):
        hot = jnp.where(iota((TILES, OBS), 0) == owner_ref[b], 1.0, 0.0)
        earlier = jnp.zeros((TILES, LANES), F32)
        for k in range(blocks):
            part = hot[:, k * LANES : (k + 1) * LANES]
            rows.append(jnp.concatenate([part, earlier], axis=1).astype(BF16))
            earlier = earlier + part
        hots.append(hot)
    counts = dot(jnp.concatenate(rows, axis=0), count)
    found = []
    for b, hot in enumerate(hots):
        first = b * blocks * TILES
        wide = jnp.concatenate(
            [counts[first + k * TILES : first + (k + 1) * TILES] for k in range(blocks)], axis=1
        )
        found.append((hot, jnp.sum(hot * wide, axis=0, keepdims=True)))
    return found


def pick_kernel(x_ref, owner_ref, field_ref, stack_ref, message_ref,
                in_ref, new_ref, fields_ref, stacks_ref, values_ref, in_sems, out_sems):
    width = GROUP * LANES
    loads = [
        pltpu.make_async_copy(
            x_ref.at[0, :, pl.ds(i * width, width)], in_ref.at[i], in_sems.at[i]
        )
        for i in range(GROUPS)
    ]
    for load in loads:
        load.start()

    slot_of = lax.bitwise_and(iota((LANES, OBS), 0), SLOTS - 1)
    fields = jnp.zeros((TILES, LANES), F32)
    stacks = jnp.zeros((TILES, LANES), F32)
    orders = owner_orders(owner_ref)
    for b, (hot, order) in enumerate(orders):
        slot_hot = slot_of == order.astype(jnp.int32) + b * OWN_MAX
        hot = hot.astype(BF16)
        of_slot = jnp.where(slot_hot, field_ref[b : b + 1, :].astype(F32), 0.0).astype(BF16)
        fields = fields + dot_nt(hot, of_slot)
        of_slot = jnp.where(slot_hot, stack_ref[b : b + 1, :].astype(F32), 0.0).astype(BF16)
        stacks = stacks + dot_nt(hot, of_slot)
    fields_ref[...] = fields
    stacks_ref[...] = stacks

    left = iota((1, LANES), 1) < SLOTS
    column_of = iota((2 * LANES, LANES), 0).astype(F32).astype(BF16)
    field_of = iota((FIELDS, LANES), 0).astype(F32)
    row_of = iota((8, LANES), 0)
    stores = []
    for group in range(GROUPS):
        loads[group].wait()
        block_ref = in_ref.at[group]
        for i in range(GROUP):
            new_ref[group * GROUP + i, 0:BULK, :] = block_ref[0:BULK, i * LANES : (i + 1) * LANES]
        stores.append(
            pltpu.make_async_copy(
                new_ref.at[pl.ds(group * GROUP, GROUP), pl.ds(0, BULK), :],
                message_ref.at[pl.ds(group * GROUP, GROUP), pl.ds(0, BULK), :],
                out_sems.at[group],
            )
        )
        stores[-1].start()
        for i in range(GROUP // 2):
            tile = group * GROUP + 2 * i
            first, second = stacks_ref[tile : tile + 1, :], stacks_ref[tile + 1 : tile + 2, :]
            column = jnp.where(left, first, second + float(LANES)).astype(BF16)
            hot = jnp.where(column_of == column, jnp.ones((), BF16), jnp.zeros((), BF16))
            by_field = dot(block_ref[:, 2 * i * LANES : (2 * i + 2) * LANES], hot)
            first, second = fields_ref[tile : tile + 1, :], fields_ref[tile + 1 : tile + 2, :]
            field = jnp.where(left, first, second)
            values_ref[tile // 2 : tile // 2 + 1, :] = jnp.sum(
                jnp.where(field_of == field, by_field, 0.0), axis=0, keepdims=True
            )

    order = orders[0][1]
    values = values_ref[...]
    turned = values.T.astype(BF16)
    by_slot = jnp.zeros((OWN_MAX, OBS), F32)
    for k in range(2):
        hot = jnp.where(2 * iota((PAIRS, OBS), 0) + k == owner_ref[0], 1.0, 0.0).astype(BF16)
        by_slot = by_slot + dot(turned[k * SLOTS : k * SLOTS + OWN_MAX], hot)
    slot_hot = iota((OWN_MAX, OBS), 0).astype(F32) == order
    first = jnp.sum(jnp.where(slot_hot, by_slot, 0.0), axis=0, keepdims=True)
    base = jnp.zeros((8, LANES), F32)
    for k in range(OBS // LANES):
        base = jnp.where(row_of == k + REST + 1, first[:, k * LANES : (k + 1) * LANES], base)
    for group in range(GROUPS):
        rest = jnp.concatenate(
            [in_ref[group, BULK:, :].astype(F32), jnp.zeros((8 - REST, width), F32)], axis=0
        )
        for i in range(GROUP):
            tile = group * GROUP + i
            end = jnp.where(
                row_of == REST,
                values[tile // 2 : tile // 2 + 1],
                rest[:, i * LANES : (i + 1) * LANES] + base,
            )
            new_ref[tile, BULK:, :] = end.astype(BF16)
    stores.append(
        pltpu.make_async_copy(
            new_ref.at[:, pl.ds(BULK, 8), :],
            message_ref.at[:, pl.ds(BULK, 8), :],
            out_sems.at[GROUPS],
        )
    )
    stores[-1].start()
    for store in stores:
        store.wait()


def pick(x, owner, field, stack):
    vmem = pl.BlockSpec(memory_space=pltpu.VMEM)
    return pl.pallas_call(
        pick_kernel,
        in_specs=[pl.BlockSpec(memory_space=pl.ANY), vmem, vmem, vmem],
        out_specs=pl.BlockSpec(memory_space=pl.ANY),
        out_shape=jax.ShapeDtypeStruct((TILES, SENT, LANES), BF16),
        scratch_shapes=[
            pltpu.VMEM((GROUPS, FIELDS, GROUP * LANES), BF16),
            pltpu.VMEM((TILES, SENT, LANES), BF16),
            pltpu.VMEM((TILES, LANES), F32),
            pltpu.VMEM((TILES, LANES), F32),
            pltpu.VMEM((PAIRS, LANES), F32),
            pltpu.SemaphoreType.DMA((GROUPS,)),
            pltpu.SemaphoreType.DMA((GROUPS + 1,)),
        ],
        compiler_params=pltpu.CompilerParams(vmem_limit_bytes=63_000_000),
    )(x, owner, field, stack)


def column(row):
    eye = iota((LANES, LANES), 0) == iota((LANES, LANES), 1)
    return jnp.broadcast_to(
        jnp.sum(jnp.where(eye, row, 0.0), axis=1, keepdims=True), (LANES, LANES)
    )


def lists_kernel(used_ref, owner_ref, roster_ref, there_ref, kind_ref, reading_ref, variance_ref,
                 weight_ref, observed_ref, noise_ref, listed_ref, near_ref, slot_ref,
                 slot_there_ref):
    core = lax.rem(lax.axis_index("tile"), 2).astype(F32)
    eye = iota((LANES, LANES), 0) == iota((LANES, LANES), 1)
    for b, (_, order) in enumerate(owner_orders(owner_ref)):
        listed = column(roster_ref[b].astype(F32))
        kind = column(kind_ref[b].astype(F32))
        listed_ref[b] = listed.astype(jnp.int32)
        taper = jnp.where(kind > 0.0, (CLASSES + 1 - kind) / CLASSES, 0.0)
        weight_ref[b] = jnp.where(listed < used_ref[b].astype(F32), taper, 0.0)
        owner = owner_ref[b]
        side = lax.bitwise_and(owner, 1).astype(F32)
        slot = lax.shift_right_logical(owner, 1).astype(F32) * OWN_MAX + order

        def hot_of(listed):
            wide = jnp.concatenate([listed] * (OBS // LANES), axis=1)
            return wide == iota((LANES, OBS), 1).astype(F32)

        hot = hot_of(listed)

        def look_up(row, hot=hot):
            return jnp.sum(jnp.where(hot, row, 0.0), axis=1, keepdims=True)

        def slots(hot):
            row = jnp.sum(jnp.where(eye, look_up(slot, hot), 0.0), axis=0, keepdims=True)
            return row.astype(jnp.int32)

        observed_ref[b] = jnp.broadcast_to(look_up(reading_ref[b : b + 1, :]), (LANES, LANES))
        noise_ref[b] = jnp.broadcast_to(look_up(variance_ref[b : b + 1, :]), (LANES, LANES))
        near_ref[b] = jnp.broadcast_to(
            jnp.where(look_up(side) == core, 1.0, 0.0), (LANES, LANES)
        )
        slot_ref[b : b + 1, :] = slots(hot)
        slot_there_ref[b : b + 1, :] = slots(hot_of(column(there_ref[b].astype(F32))))


def lists(used, owner, roster, there, kind, reading, variance):
    vmem = pl.BlockSpec(memory_space=pltpu.VMEM)
    square = jax.ShapeDtypeStruct((BATCHES, LANES, LANES), F32)
    return pl.pallas_call(
        lists_kernel,
        in_specs=[pl.BlockSpec(memory_space=pltpu.SMEM)] + [vmem] * 6,
        out_specs=[vmem] * 7,
        out_shape=[square, square, square, jax.ShapeDtypeStruct(square.shape, jnp.int32), square,
                   jax.ShapeDtypeStruct((BATCHES, LANES), jnp.int32),
                   jax.ShapeDtypeStruct((BATCHES, LANES), jnp.int32)],
        compiler_params=pltpu.CompilerParams(vmem_limit_bytes=VMEM_LIMIT),
    )(used, owner, roster, there, kind, reading, variance)


def coded(x):
    size = CODES_PER_OCTAVE * jnp.log2(1.0 + jnp.abs(x) * (1.0 / FINEST))
    return jnp.round(jnp.where(x < 0.0, -size, size)).astype(jnp.int32).astype(jnp.int16)


def decoded(code):
    size = jnp.exp2(jnp.abs(code) * (1.0 / CODES_PER_OCTAVE)) - 1.0
    return jnp.where(code < 0.0, -FINEST, FINEST) * size


def transform_of(prior, weight, observed, noise):
    eye = jnp.where(iota((LANES, LANES), 0) == iota((LANES, LANES), 1), 1.0, 0.0)
    mean = jnp.sum(prior, axis=1, keepdims=True) * (1.0 / MEMBERS)
    scaled = weight * (prior - mean) * INVERSE_ROOT
    inverse_noise = 1.0 / noise
    right = jnp.concatenate(
        [scaled * inverse_noise, weight * (observed - mean) * inverse_noise], axis=1
    )
    both = dot(scaled.T, right, HIGHEST)
    matrix = both[:, :LANES] + eye
    pull = both[:, LANES:]
    bound = jnp.max(jnp.sum(jnp.abs(matrix), axis=0, keepdims=True)) * 1.00001
    scale = 2.0 / (1.0 + bound)
    rho = (bound - 1.0) / (bound + 1.0)

    def unfinished(carry):
        return carry[0] > 3e-4

    def square(carry):
        rho, x, e = carry
        gain = 2.0 / (2.0 - rho * rho)
        products = dot(jnp.concatenate([x, e], axis=0), e, lax.Precision.HIGH)
        x = gain * (x + products[:LANES])
        e = gain * products[LANES:] + (1.0 - gain) * eye
        return rho * rho / (2.0 - rho * rho), x, e

    _, inverse, _ = lax.while_loop(unfinished, square, (rho, scale * eye, eye - scale * matrix))

    def refine(_, x):
        return x + dot(x, eye - dot(matrix, x, HIGHEST), HIGHEST)

    inverse = lax.fori_loop(0, jnp.where(bound > 200.0, 2, 1), refine, inverse)
    return 0.5 * (eye + inverse) + dot(inverse, pull, HIGHEST) * INVERSE_ROOT


def first_kernel(message_ref, listed_ref, weight_ref, observed_ref, noise_ref,
                 sent_ref, total_ref, own_ref, scratch_ref):
    odd = lax.rem(lax.axis_index("tile"), 2) == 1
    scratch_ref[...] = message_ref[:, 0:8, :].astype(F32).reshape(MEMBERS * 8, LANES)
    listed = listed_ref[0]
    values = jnp.concatenate(
        [
            scratch_ref[pl.ds(REST + 1 + k, MEMBERS, stride=8), :].astype(BF16)
            for k in range(OBS // LANES)
        ],
        axis=1,
    )
    hot = jnp.concatenate(
        [
            jnp.where(listed == iota((LANES, LANES), 1) + k * LANES, 1.0, 0.0).astype(BF16)
            for k in range(OBS // LANES)
        ],
        axis=1,
    )
    prior = dot_nt(hot, values)
    pair = scratch_ref[pl.ds(REST, MEMBERS, stride=8), :].T
    own = jnp.where(odd, pair[SLOTS + OWN_MAX :], pair[OWN_MAX:SLOTS])
    transform = transform_of(prior, weight_ref[0], observed_ref[0], noise_ref[0])
    own = dot(own, transform, HIGHEST)
    own_ref[...] = own[OWN_MAX:]
    total_ref[...] = transform
    sent_ref[...] = jnp.broadcast_to(
        coded(own[:OWN_MAX])[None], (PAIRS, OWN_MAX, LANES)
    )


def prior_of(side_ref, near_ref, far_ref):
    near = near_ref[...].astype(jnp.int32).astype(F32)
    far = far_ref[...].astype(jnp.int32).astype(F32)
    return decoded(jnp.where(side_ref[0] > 0.0, near, far))


def next_kernel(near_ref, far_ref, side_ref, weight_ref, observed_ref, noise_ref, own_ref,
                total_ref, sent_ref, total_out_ref, *rest_ref):
    prior = prior_of(side_ref, near_ref, far_ref)
    transform = transform_of(prior, weight_ref[0], observed_ref[0], noise_ref[0])
    left = own_ref.shape[0]
    new = dot(jnp.concatenate([own_ref[...], total_ref[...]], axis=0), transform, HIGHEST)
    sent_ref[...] = jnp.broadcast_to(coded(new[:OWN_MAX])[None], (PAIRS, OWN_MAX, LANES))
    if left > OWN_MAX:
        rest_ref[0][...] = new[OWN_MAX:left]
    total_out_ref[...] = new[left:]


def whole(*shape):
    return pl.BlockSpec(shape, lambda i: (0,) * len(shape))


def list_blocks(b, number):
    return [pl.BlockSpec((1, LANES, LANES), lambda i: (b, 0, 0))] * number


def solve(b, near, far, lists_of, own=None, total=None):
    weight, observed, noise, listed, side = lists_of[:5]
    left = (BATCHES - 2 - b) * OWN_MAX
    out_shape = [
        jax.ShapeDtypeStruct((PAIRS, OWN_MAX, LANES), jnp.int16),
        jax.ShapeDtypeStruct((LANES, LANES), F32),
    ]
    if left:
        out_shape.append(jax.ShapeDtypeStruct((left, LANES), F32))
    params = pltpu.CompilerParams(vmem_limit_bytes=VMEM_LIMIT)
    cost = pl.CostEstimate(flops=400_000_000, bytes_accessed=4_000_000, transcendentals=0)
    if b == 0:
        kernel, scratch = first_kernel, [pltpu.VMEM((MEMBERS * 8, LANES), F32)]
        operands = (near, listed, weight, observed, noise)
        in_specs = [
            pl.BlockSpec((MEMBERS, 16, LANES), lambda i: (0, BULK // 16, 0))
        ] + list_blocks(b, 4)
    else:
        kernel, scratch = next_kernel, []
        operands = (near, far, side, weight, observed, noise, own, total)
        in_specs = (
            [whole(LANES, LANES)] * 2
            + list_blocks(b, 4)
            + [whole(*own.shape), whole(LANES, LANES)]
        )
    sent, total, *own = pl.pallas_call(
        kernel,
        grid=(1,),
        in_specs=in_specs,
        out_specs=[whole(*s.shape) for s in out_shape],
        out_shape=out_shape,
        scratch_shapes=scratch,
        compiler_params=params,
        cost_estimate=cost,
    )(*operands)
    return sent, own[0] if own else None, total


def select_kernel(b, slot_ref, rows_ref, out_ref, wide_ref, found_ref):
    wide_ref[...] = rows_ref[...].astype(jnp.int32)
    for slot in range(LANES):
        found_ref[slot : slot + 1, :] = wide_ref[pl.ds(slot_ref[b, slot], 1), :]
    out_ref[...] = found_ref[...].astype(jnp.int16)


def select(b, slots, rows):
    return pl.pallas_call(
        functools.partial(select_kernel, b),
        grid=(1,),
        in_specs=[pl.BlockSpec(memory_space=pltpu.SMEM), whole(PAIRS * OWN_MAX, LANES)],
        out_specs=whole(LANES, LANES),
        out_shape=jax.ShapeDtypeStruct((LANES, LANES), jnp.int16),
        scratch_shapes=[
            pltpu.VMEM((PAIRS * OWN_MAX, LANES), jnp.int32),
            pltpu.VMEM((LANES, LANES), jnp.int32),
        ],
        compiler_params=pltpu.CompilerParams(vmem_limit_bytes=VMEM_LIMIT),
        cost_estimate=pl.CostEstimate(flops=0, bytes_accessed=1_000_000, transcendentals=0),
    )(slots, rows)


ROWS = 32
CHUNKS = BULK // ROWS
LOADS = 8


def last_kernel(near_ref, far_ref, side_ref, weight_ref, observed_ref, noise_ref, total_ref, x_ref,
                out_ref, in_ref, new_ref, flat_ref, in_sems, out_sems):
    share = MEMBERS // LOADS
    loads = [
        pltpu.make_async_copy(
            x_ref.at[pl.ds(i * share, share)], in_ref.at[pl.ds(i * share, share)], in_sems.at[i]
        )
        for i in range(LOADS)
    ]
    for load in loads:
        load.start()
    prior = prior_of(side_ref, near_ref, far_ref)
    transform = transform_of(prior, weight_ref[0], observed_ref[0], noise_ref[0])
    exact = dot(total_ref[...], transform, HIGHEST).T
    high = exact.astype(BF16)
    total = jnp.concatenate([high, (exact - high.astype(F32)).astype(BF16)], axis=1)

    def spread(i, part, parts):
        held = min(ROWS, SENT - i * ROWS)
        members = slice(part * MEMBERS // parts, (part + 1) * MEMBERS // parts)
        rows = in_ref[members, i * ROWS : i * ROWS + held, :]
        flat_ref[i % 2, members, 0:held, :] = rows.astype(F32)

    def row(i, v):
        rows_ref = flat_ref.at[i % 2].reshape(MEMBERS * (ROWS + 8), LANES)
        return rows_ref[pl.ds(v, MEMBERS, stride=ROWS + 8), :].astype(BF16)

    def transformed(x):
        return dot(total, jnp.concatenate([x, x], axis=0)).astype(BF16)

    for part, load in enumerate(loads):
        load.wait()
        spread(0, part, LOADS)
    stores = []
    for i in range(CHUNKS + 1):
        first, number = i * ROWS, (ROWS if i < CHUNKS else REST)
        for v in range(0, number, 2):
            if i < CHUNKS:
                spread(i + 1, v // 2, ROWS // 2)
            y = transformed(jnp.concatenate([row(i, v), row(i, v + 1)], axis=1))
            for k in range(min(2, number - v)):
                new_ref[first + v + k] = y[:, k * LANES : (k + 1) * LANES]
        places = pl.ds(first, number)
        stores.append(
            pltpu.make_async_copy(new_ref.at[places], out_ref.at[places], out_sems.at[i])
        )
        stores[-1].start()
    for store in stores:
        store.wait()


def finish(near, far, lists_of, total, x):
    b = BATCHES - 1
    weight, observed, noise, _, side = lists_of[:5]
    return pl.pallas_call(
        last_kernel,
        grid=(1,),
        in_specs=[whole(LANES, LANES)] * 2
        + list_blocks(b, 4)
        + [whole(LANES, LANES), pl.BlockSpec(memory_space=pl.ANY)],
        out_specs=pl.BlockSpec(memory_space=pl.ANY),
        out_shape=jax.ShapeDtypeStruct((FIELDS, MEMBERS, LANES), BF16),
        scratch_shapes=[
            pltpu.VMEM((MEMBERS, SENT, LANES), BF16),
            pltpu.VMEM((FIELDS, MEMBERS, LANES), BF16),
            pltpu.VMEM((2, MEMBERS, ROWS + 8, LANES), F32),
            pltpu.SemaphoreType.DMA((LOADS,)),
            pltpu.SemaphoreType.DMA((CHUNKS + 1,)),
        ],
        compiler_params=pltpu.CompilerParams(vmem_limit_bytes=24 * 1024 * 1024),
    )(near, far, side, weight, observed, noise, total, x)


def exchange(x, groups=None):
    return lax.all_to_all(x, AXES, split_axis=0, concat_axis=0, axis_index_groups=groups)


def to_chips(x):
    return exchange(x, [list(range(core, TILES, 2)) for core in range(2)])


def swap(x):
    size = lax.axis_size("tile")
    return lax.ppermute(x, "tile", [(i, i ^ 1) for i in range(size)])


def local(
    background_sample,
    measured_reading,
    measurement_noise_variance,
    measurements_in_batch,
    measurement_patch,
    measurement_stack,
    measured_field,
    patch_measurement_roster,
    entry_damping_kind,
):
    owner = measurement_patch.reshape(BATCHES, 1, OBS)
    roster_there = swap(patch_measurement_roster)
    message = pick(background_sample, owner, measured_field, measurement_stack)
    message, used = lax.optimization_barrier((message, measurements_in_batch))
    lists_of = lists(
        used, owner, patch_measurement_roster, roster_there, entry_damping_kind,
        measured_reading, measurement_noise_variance,
    )
    fields, lists_of = lax.optimization_barrier((exchange(message), lists_of))
    slots, slots_there = lists_of[-2:]
    sent, own, total = solve(0, fields, None, lists_of)
    for b in range(1, BATCHES):
        rows = to_chips(sent).reshape(PAIRS * OWN_MAX, LANES)
        far = swap(select(b, slots_there, rows))
        near = select(b, slots, rows)
        if b < BATCHES - 1:
            sent, own, total = solve(b, near, far, lists_of, own, total)
    return finish(near, far, lists_of, total, fields).transpose(1, 0, 2)


def solution(mesh):
    in_specs = (
        P(AXES, None, None),
        P(),
        P(),
        P(),
        P(),
        P(),
        P(),
        P(None, AXES, None),
        P(None, AXES, None),
    )
    out_specs = P(None, None, AXES)
    return jax.shard_map(local, mesh=mesh, in_specs=in_specs, out_specs=out_specs, check_vma=False)
```

```python
import functools
import jax
import jax.numpy as jnp
from jax import lax
from jax.experimental import pallas as pl
from jax.experimental.pallas import tpu as pltpu
from jax.sharding import PartitionSpec as P

OWN_MAX = 16
CLASSES = 8
AXES = ("mem", "tile")
BATCHES = 4
OBS = 512
TILES = 128
MEMBERS = 128
LANES = 128
FIELDS = 227
REST = 3
BULK = FIELDS - REST
SENT = BULK + 8
SLOTS = BATCHES * OWN_MAX
GROUP = 16
PAIRS = TILES // 2
GROUPS = TILES // GROUP
VMEM_LIMIT = 16 * 1024 * 1024
HIGHEST = lax.Precision.HIGHEST
F32 = jnp.float32
FINEST = 0.25
CODES_PER_OCTAVE = 1326.0
BF16 = jnp.bfloat16
INVERSE_ROOT = 1.0 / (MEMBERS - 1) ** 0.5


def iota(shape, dim):
    return lax.broadcasted_iota(jnp.int32, shape, dim)


def dot(a, b, precision=None):
    return jnp.dot(a, b, precision=precision, preferred_element_type=F32)


def dot_nt(a, b):
    return lax.dot_general(a, b, (((1,), (1,)), ((), ())), preferred_element_type=F32)


def owner_orders(owner_ref):
    before = jnp.where(iota((LANES, LANES), 0) < iota((LANES, LANES), 1), 1.0, 0.0).astype(BF16)
    count = jnp.concatenate([before, jnp.ones((LANES, LANES), BF16)], axis=0)
    blocks = OBS // LANES
    hots, rows = [], []
    for b in range(BATCHES):
        hot = jnp.where(iota((TILES, OBS), 0) == owner_ref[b], 1.0, 0.0)
        earlier = jnp.zeros((TILES, LANES), F32)
        for k in range(blocks):
            part = hot[:, k * LANES : (k + 1) * LANES]
            rows.append(jnp.concatenate([part, earlier], axis=1).astype(BF16))
            earlier = earlier + part
        hots.append(hot)
    counts = dot(jnp.concatenate(rows, axis=0), count)
    found = []
    for b, hot in enumerate(hots):
        first = b * blocks * TILES
        wide = jnp.concatenate(
            [counts[first + k * TILES : first + (k + 1) * TILES] for k in range(blocks)], axis=1
        )
        found.append((hot, jnp.sum(hot * wide, axis=0, keepdims=True)))
    return found


def pick_kernel(x_ref, owner_ref, field_ref, stack_ref, message_ref,
                in_ref, new_ref, fields_ref, stacks_ref, values_ref, in_sems, out_sems):
    width = GROUP * LANES
    loads = [
        pltpu.make_async_copy(
            x_ref.at[0, :, pl.ds(i * width, width)], in_ref.at[i], in_sems.at[i]
        )
        for i in range(GROUPS)
    ]
    for load in loads:
        load.start()

    slot_of = lax.bitwise_and(iota((LANES, OBS), 0), SLOTS - 1)
    fields = jnp.zeros((TILES, LANES), F32)
    stacks = jnp.zeros((TILES, LANES), F32)
    orders = owner_orders(owner_ref)
    for b, (hot, order) in enumerate(orders):
        slot_hot = slot_of == order.astype(jnp.int32) + b * OWN_MAX
        hot = hot.astype(BF16)
        of_slot = jnp.where(slot_hot, field_ref[b : b + 1, :].astype(F32), 0.0).astype(BF16)
        fields = fields + dot_nt(hot, of_slot)
        of_slot = jnp.where(slot_hot, stack_ref[b : b + 1, :].astype(F32), 0.0).astype(BF16)
        stacks = stacks + dot_nt(hot, of_slot)
    fields_ref[...] = fields
    stacks_ref[...] = stacks

    left = iota((1, LANES), 1) < SLOTS
    column_of = iota((2 * LANES, LANES), 0).astype(F32).astype(BF16)
    field_of = iota((FIELDS, LANES), 0).astype(F32)
    row_of = iota((8, LANES), 0)
    stores = []
    for group in range(GROUPS):
        loads[group].wait()
        block_ref = in_ref.at[group]
        for i in range(GROUP):
            new_ref[group * GROUP + i, 0:BULK, :] = block_ref[0:BULK, i * LANES : (i + 1) * LANES]
        stores.append(
            pltpu.make_async_copy(
                new_ref.at[pl.ds(group * GROUP, GROUP), pl.ds(0, BULK), :],
                message_ref.at[pl.ds(group * GROUP, GROUP), pl.ds(0, BULK), :],
                out_sems.at[group],
            )
        )
        stores[-1].start()
        for i in range(GROUP // 2):
            tile = group * GROUP + 2 * i
            first, second = stacks_ref[tile : tile + 1, :], stacks_ref[tile + 1 : tile + 2, :]
            column = jnp.where(left, first, second + float(LANES)).astype(BF16)
            hot = jnp.where(column_of == column, jnp.ones((), BF16), jnp.zeros((), BF16))
            by_field = dot(block_ref[:, 2 * i * LANES : (2 * i + 2) * LANES], hot)
            first, second = fields_ref[tile : tile + 1, :], fields_ref[tile + 1 : tile + 2, :]
            field = jnp.where(left, first, second)
            values_ref[tile // 2 : tile // 2 + 1, :] = jnp.sum(
                jnp.where(field_of == field, by_field, 0.0), axis=0, keepdims=True
            )

    order = orders[0][1]
    values = values_ref[...]
    turned = values.T.astype(BF16)
    by_slot = jnp.zeros((OWN_MAX, OBS), F32)
    for k in range(2):
        hot = jnp.where(2 * iota((PAIRS, OBS), 0) + k == owner_ref[0], 1.0, 0.0).astype(BF16)
        by_slot = by_slot + dot(turned[k * SLOTS : k * SLOTS + OWN_MAX], hot)
    slot_hot = iota((OWN_MAX, OBS), 0).astype(F32) == order
    first = jnp.sum(jnp.where(slot_hot, by_slot, 0.0), axis=0, keepdims=True)
    base = jnp.zeros((8, LANES), F32)
    for k in range(OBS // LANES):
        base = jnp.where(row_of == k + REST + 1, first[:, k * LANES : (k + 1) * LANES], base)
    for group in range(GROUPS):
        rest = jnp.concatenate(
            [in_ref[group, BULK:, :].astype(F32), jnp.zeros((8 - REST, width), F32)], axis=0
        )
        for i in range(GROUP):
            tile = group * GROUP + i
            end = jnp.where(
                row_of == REST,
                values[tile // 2 : tile // 2 + 1],
                rest[:, i * LANES : (i + 1) * LANES] + base,
            )
            new_ref[tile, BULK:, :] = end.astype(BF16)
    stores.append(
        pltpu.make_async_copy(
            new_ref.at[:, pl.ds(BULK, 8), :],
            message_ref.at[:, pl.ds(BULK, 8), :],
            out_sems.at[GROUPS],
        )
    )
    stores[-1].start()
    for store in stores:
        store.wait()


def pick(x, owner, field, stack):
    vmem = pl.BlockSpec(memory_space=pltpu.VMEM)
    return pl.pallas_call(
        pick_kernel,
        in_specs=[pl.BlockSpec(memory_space=pl.ANY), vmem, vmem, vmem],
        out_specs=pl.BlockSpec(memory_space=pl.ANY),
        out_shape=jax.ShapeDtypeStruct((TILES, SENT, LANES), BF16),
        scratch_shapes=[
            pltpu.VMEM((GROUPS, FIELDS, GROUP * LANES), BF16),
            pltpu.VMEM((TILES, SENT, LANES), BF16),
            pltpu.VMEM((TILES, LANES), F32),
            pltpu.VMEM((TILES, LANES), F32),
            pltpu.VMEM((PAIRS, LANES), F32),
            pltpu.SemaphoreType.DMA((GROUPS,)),
            pltpu.SemaphoreType.DMA((GROUPS + 1,)),
        ],
        compiler_params=pltpu.CompilerParams(vmem_limit_bytes=63_000_000),
    )(x, owner, field, stack)


def column(row):
    eye = iota((LANES, LANES), 0) == iota((LANES, LANES), 1)
    return jnp.broadcast_to(
        jnp.sum(jnp.where(eye, row, 0.0), axis=1, keepdims=True), (LANES, LANES)
    )


def lists_kernel(used_ref, owner_ref, roster_ref, there_ref, kind_ref, reading_ref, variance_ref,
                 weight_ref, observed_ref, noise_ref, listed_ref, near_ref, slot_ref,
                 slot_there_ref):
    core = lax.rem(lax.axis_index("tile"), 2).astype(F32)
    eye = iota((LANES, LANES), 0) == iota((LANES, LANES), 1)
    for b, (_, order) in enumerate(owner_orders(owner_ref)):
        listed = column(roster_ref[b].astype(F32))
        kind = column(kind_ref[b].astype(F32))
        listed_ref[b] = listed.astype(jnp.int32)
        taper = jnp.where(kind > 0.0, (CLASSES + 1 - kind) / CLASSES, 0.0)
        weight_ref[b] = jnp.where(listed < used_ref[b].astype(F32), taper, 0.0)
        owner = owner_ref[b]
        side = lax.bitwise_and(owner, 1).astype(F32)
        slot = lax.shift_right_logical(owner, 1).astype(F32) * OWN_MAX + order

        def hot_of(listed):
            wide = jnp.concatenate([listed] * (OBS // LANES), axis=1)
            return wide == iota((LANES, OBS), 1).astype(F32)

        hot = hot_of(listed)

        def look_up(row, hot=hot):
            return jnp.sum(jnp.where(hot, row, 0.0), axis=1, keepdims=True)

        def slots(hot):
            row = jnp.sum(jnp.where(eye, look_up(slot, hot), 0.0), axis=0, keepdims=True)
            return row.astype(jnp.int32)

        observed_ref[b] = jnp.broadcast_to(look_up(reading_ref[b : b + 1, :]), (LANES, LANES))
        noise_ref[b] = jnp.broadcast_to(look_up(variance_ref[b : b + 1, :]), (LANES, LANES))
        near_ref[b] = jnp.broadcast_to(
            jnp.where(look_up(side) == core, 1.0, 0.0), (LANES, LANES)
        )
        slot_ref[b : b + 1, :] = slots(hot)
        slot_there_ref[b : b + 1, :] = slots(hot_of(column(there_ref[b].astype(F32))))


def lists(used, owner, roster, there, kind, reading, variance):
    vmem = pl.BlockSpec(memory_space=pltpu.VMEM)
    square = jax.ShapeDtypeStruct((BATCHES, LANES, LANES), F32)
    return pl.pallas_call(
        lists_kernel,
        in_specs=[pl.BlockSpec(memory_space=pltpu.SMEM)] + [vmem] * 6,
        out_specs=[vmem] * 7,
        out_shape=[square, square, square, jax.ShapeDtypeStruct(square.shape, jnp.int32), square,
                   jax.ShapeDtypeStruct((BATCHES, LANES), jnp.int32),
                   jax.ShapeDtypeStruct((BATCHES, LANES), jnp.int32)],
        compiler_params=pltpu.CompilerParams(vmem_limit_bytes=VMEM_LIMIT),
    )(used, owner, roster, there, kind, reading, variance)


def coded(x):
    size = CODES_PER_OCTAVE * jnp.log2(1.0 + jnp.abs(x) * (1.0 / FINEST))
    return jnp.round(jnp.where(x < 0.0, -size, size)).astype(jnp.int32).astype(jnp.int16)


def decoded(code):
    size = jnp.exp2(jnp.abs(code) * (1.0 / CODES_PER_OCTAVE)) - 1.0
    return jnp.where(code < 0.0, -FINEST, FINEST) * size


def transform_of(prior, weight, observed, noise):
    eye = jnp.where(iota((LANES, LANES), 0) == iota((LANES, LANES), 1), 1.0, 0.0)
    mean = jnp.sum(prior, axis=1, keepdims=True) * (1.0 / MEMBERS)
    scaled = weight * (prior - mean) * INVERSE_ROOT
    inverse_noise = 1.0 / noise
    right = jnp.concatenate(
        [scaled * inverse_noise, weight * (observed - mean) * inverse_noise], axis=1
    )
    both = dot(scaled.T, right, HIGHEST)
    matrix = both[:, :LANES] + eye
    pull = both[:, LANES:]
    bound = jnp.max(jnp.sum(jnp.abs(matrix), axis=0, keepdims=True)) * 1.00001
    scale = 2.0 / (1.0 + bound)
    rho = (bound - 1.0) / (bound + 1.0)

    def unfinished(carry):
        return carry[0] > 3e-4

    def square(carry):
        rho, x, e = carry
        gain = 2.0 / (2.0 - rho * rho)
        products = dot(jnp.concatenate([x, e], axis=0), e, lax.Precision.HIGH)
        x = gain * (x + products[:LANES])
        e = gain * products[LANES:] + (1.0 - gain) * eye
        return rho * rho / (2.0 - rho * rho), x, e

    _, inverse, _ = lax.while_loop(unfinished, square, (rho, scale * eye, eye - scale * matrix))

    def refine(_, x):
        return x + dot(x, eye - dot(matrix, x, HIGHEST), HIGHEST)

    inverse = lax.fori_loop(0, jnp.where(bound > 200.0, 2, 1), refine, inverse)
    return 0.5 * (eye + inverse) + dot(inverse, pull, HIGHEST) * INVERSE_ROOT


def first_kernel(message_ref, listed_ref, weight_ref, observed_ref, noise_ref,
                 sent_ref, total_ref, own_ref, scratch_ref):
    odd = lax.rem(lax.axis_index("tile"), 2) == 1
    scratch_ref[...] = message_ref[:, 0:8, :].astype(F32).reshape(MEMBERS * 8, LANES)
    listed = listed_ref[0]
    values = jnp.concatenate(
        [
            scratch_ref[pl.ds(REST + 1 + k, MEMBERS, stride=8), :].astype(BF16)
            for k in range(OBS // LANES)
        ],
        axis=1,
    )
    hot = jnp.concatenate(
        [
            jnp.where(listed == iota((LANES, LANES), 1) + k * LANES, 1.0, 0.0).astype(BF16)
            for k in range(OBS // LANES)
        ],
        axis=1,
    )
    prior = dot_nt(hot, values)
    pair = scratch_ref[pl.ds(REST, MEMBERS, stride=8), :].T
    own = jnp.where(odd, pair[SLOTS + OWN_MAX :], pair[OWN_MAX:SLOTS])
    transform = transform_of(prior, weight_ref[0], observed_ref[0], noise_ref[0])
    own = dot(own, transform, HIGHEST)
    own_ref[...] = own[OWN_MAX:]
    total_ref[...] = transform
    sent_ref[...] = jnp.broadcast_to(
        coded(own[:OWN_MAX])[None], (PAIRS, OWN_MAX, LANES)
    )


def prior_of(side_ref, near_ref, far_ref):
    near = near_ref[...].astype(jnp.int32).astype(F32)
    far = far_ref[...].astype(jnp.int32).astype(F32)
    return decoded(jnp.where(side_ref[0] > 0.0, near, far))


def next_kernel(near_ref, far_ref, side_ref, weight_ref, observed_ref, noise_ref, own_ref,
                total_ref, sent_ref, total_out_ref, *rest_ref):
    prior = prior_of(side_ref, near_ref, far_ref)
    transform = transform_of(prior, weight_ref[0], observed_ref[0], noise_ref[0])
    left = own_ref.shape[0]
    new = dot(jnp.concatenate([own_ref[...], total_ref[...]], axis=0), transform, HIGHEST)
    sent_ref[...] = jnp.broadcast_to(coded(new[:OWN_MAX])[None], (PAIRS, OWN_MAX, LANES))
    if left > OWN_MAX:
        rest_ref[0][...] = new[OWN_MAX:left]
    total_out_ref[...] = new[left:]


def whole(*shape):
    return pl.BlockSpec(shape, lambda i: (0,) * len(shape))


def list_blocks(b, number):
    return [pl.BlockSpec((1, LANES, LANES), lambda i: (b, 0, 0))] * number


def solve(b, near, far, lists_of, own=None, total=None):
    weight, observed, noise, listed, side = lists_of[:5]
    left = (BATCHES - 2 - b) * OWN_MAX
    out_shape = [
        jax.ShapeDtypeStruct((PAIRS, OWN_MAX, LANES), jnp.int16),
        jax.ShapeDtypeStruct((LANES, LANES), F32),
    ]
    if left:
        out_shape.append(jax.ShapeDtypeStruct((left, LANES), F32))
    params = pltpu.CompilerParams(vmem_limit_bytes=VMEM_LIMIT)
    cost = pl.CostEstimate(flops=400_000_000, bytes_accessed=4_000_000, transcendentals=0)
    if b == 0:
        kernel, scratch = first_kernel, [pltpu.VMEM((MEMBERS * 8, LANES), F32)]
        operands = (near, listed, weight, observed, noise)
        in_specs = [
            pl.BlockSpec((MEMBERS, 16, LANES), lambda i: (0, BULK // 16, 0))
        ] + list_blocks(b, 4)
    else:
        kernel, scratch = next_kernel, []
        operands = (near, far, side, weight, observed, noise, own, total)
        in_specs = (
            [whole(LANES, LANES)] * 2
            + list_blocks(b, 4)
            + [whole(*own.shape), whole(LANES, LANES)]
        )
    sent, total, *own = pl.pallas_call(
        kernel,
        grid=(1,),
        in_specs=in_specs,
        out_specs=[whole(*s.shape) for s in out_shape],
        out_shape=out_shape,
        scratch_shapes=scratch,
        compiler_params=params,
        cost_estimate=cost,
    )(*operands)
    return sent, own[0] if own else None, total


def select_kernel(b, slot_ref, rows_ref, out_ref, wide_ref, found_ref):
    wide_ref[...] = rows_ref[...].astype(jnp.int32)
    for slot in range(LANES):
        found_ref[slot : slot + 1, :] = wide_ref[pl.ds(slot_ref[b, slot], 1), :]
    out_ref[...] = found_ref[...].astype(jnp.int16)


def select(b, slots, rows):
    return pl.pallas_call(
        functools.partial(select_kernel, b),
        grid=(1,),
        in_specs=[pl.BlockSpec(memory_space=pltpu.SMEM), whole(PAIRS * OWN_MAX, LANES)],
        out_specs=whole(LANES, LANES),
        out_shape=jax.ShapeDtypeStruct((LANES, LANES), jnp.int16),
        scratch_shapes=[
            pltpu.VMEM((PAIRS * OWN_MAX, LANES), jnp.int32),
            pltpu.VMEM((LANES, LANES), jnp.int32),
        ],
        compiler_params=pltpu.CompilerParams(vmem_limit_bytes=VMEM_LIMIT),
        cost_estimate=pl.CostEstimate(flops=0, bytes_accessed=1_000_000, transcendentals=0),
    )(slots, rows)


ROWS = 112
CHUNKS = BULK // ROWS


def last_kernel(near_ref, far_ref, side_ref, weight_ref, observed_ref, noise_ref, total_ref, x_ref,
                out_ref, in_ref, new_ref, in_sem, out_sems):
    load = pltpu.make_async_copy(x_ref, in_ref, in_sem)
    load.start()
    prior = prior_of(side_ref, near_ref, far_ref)
    transform = transform_of(prior, weight_ref[0], observed_ref[0], noise_ref[0])
    exact = dot(total_ref[...], transform, HIGHEST).T
    high = exact.astype(BF16)
    total = jnp.concatenate([high, (exact - high.astype(F32)).astype(BF16)], axis=1)

    def transformed(x):
        return dot(total, jnp.concatenate([x, x], axis=0)).astype(BF16)

    load.wait()
    stores = []
    for i in range(CHUNKS + 1):
        first, number = i * ROWS, (ROWS if i < CHUNKS else REST)
        for v in range(0, number, 2):
            if v % 8 == 0:
                turned = jnp.swapaxes(in_ref[:, first + v : first + v + 8, :], 0, 1)
            y = transformed(jnp.concatenate([turned[v % 8], turned[v % 8 + 1]], axis=1))
            for k in range(min(2, number - v)):
                new_ref[first + v + k] = y[:, k * LANES : (k + 1) * LANES]
        places = pl.ds(first, number)
        stores.append(
            pltpu.make_async_copy(new_ref.at[places], out_ref.at[places], out_sems.at[i])
        )
        stores[-1].start()
    for store in stores:
        store.wait()


def finish(near, far, lists_of, total, x):
    b = BATCHES - 1
    weight, observed, noise, _, side = lists_of[:5]
    return pl.pallas_call(
        last_kernel,
        grid=(1,),
        in_specs=[whole(LANES, LANES)] * 2
        + list_blocks(b, 4)
        + [whole(LANES, LANES), pl.BlockSpec(memory_space=pl.ANY)],
        out_specs=pl.BlockSpec(memory_space=pl.ANY),
        out_shape=jax.ShapeDtypeStruct((FIELDS, MEMBERS, LANES), BF16),
        scratch_shapes=[
            pltpu.VMEM((MEMBERS, SENT, LANES), BF16),
            pltpu.VMEM((FIELDS, MEMBERS, LANES), BF16),
            pltpu.SemaphoreType.DMA,
            pltpu.SemaphoreType.DMA((CHUNKS + 1,)),
        ],
        compiler_params=pltpu.CompilerParams(vmem_limit_bytes=24 * 1024 * 1024),
    )(near, far, side, weight, observed, noise, total, x)


def exchange(x, groups=None):
    return lax.all_to_all(x, AXES, split_axis=0, concat_axis=0, axis_index_groups=groups)


def to_chips(x):
    return exchange(x, [list(range(core, TILES, 2)) for core in range(2)])


def swap(x):
    size = lax.axis_size("tile")
    return lax.ppermute(x, "tile", [(i, i ^ 1) for i in range(size)])


def local(
    background_sample,
    measured_reading,
    measurement_noise_variance,
    measurements_in_batch,
    measurement_patch,
    measurement_stack,
    measured_field,
    patch_measurement_roster,
    entry_damping_kind,
):
    owner = measurement_patch.reshape(BATCHES, 1, OBS)
    roster_there = swap(patch_measurement_roster)
    message = pick(background_sample, owner, measured_field, measurement_stack)
    message, used = lax.optimization_barrier((message, measurements_in_batch))
    lists_of = lists(
        used, owner, patch_measurement_roster, roster_there, entry_damping_kind,
        measured_reading, measurement_noise_variance,
    )
    fields, lists_of = lax.optimization_barrier((exchange(message), lists_of))
    slots, slots_there = lists_of[-2:]
    sent, own, total = solve(0, fields, None, lists_of)
    for b in range(1, BATCHES):
        rows = to_chips(sent).reshape(PAIRS * OWN_MAX, LANES)
        far = swap(select(b, slots_there, rows))
        near = select(b, slots, rows)
        if b < BATCHES - 1:
            sent, own, total = solve(b, near, far, lists_of, own, total)
    return finish(near, far, lists_of, total, fields).transpose(1, 0, 2)


def solution(mesh):
    in_specs = (
        P(AXES, None, None),
        P(),
        P(),
        P(),
        P(),
        P(),
        P(),
        P(None, AXES, None),
        P(None, AXES, None),
    )
    out_specs = P(None, None, AXES)
    return jax.shard_map(local, mesh=mesh, in_specs=in_specs, out_specs=out_specs, check_vma=False)
```
